128 devices in a mesh: seq: 32 (over y, z, core), head: 4 (over x).
Axes of the slice: x: 4, y: 4, z: 4, core: 2. Of those that a mesh axis runs over, the one named last changes fastest.
Arguments:
- queries: bfloat16 [12288, 2560], P('seq', 'head'), may hold values from -24 to 24
- keys: bfloat16 [12288, 2560], P('seq', 'head'), may hold values from -8 to 8
- values: bfloat16 [12288, 2560], P('seq', 'head'), may hold values from -6 to 6
- out_grad: bfloat16 [12288, 2560], P('seq', 'head'), may hold values from -6 to 6
- out_weight: bfloat16 [2560, 2560], P('head'), may hold values from -0.125 to 0.125
- offsets: int32 [32], P('head'), may hold values from 0 to 7, as said below
Outputs:
- query_grad: bfloat16 [12288, 2560], P('seq', 'head')
- key_grad: bfloat16 [12288, 2560], P('seq', 'head')
- value_grad: bfloat16 [12288, 2560], P('seq', 'head')
The draws below stay inside these ranges and needn't reach their ends.
Inputs may be any that keep to these rules, and one draw needn't show every extreme that they name: offsets[h] is below 2 ** (h mod 4).
All inputs are finite; a program needn't handle non-finite values.
Results may differ from the reference program's by a relative error of at most 0.011.
Values may be sent and summed in bfloat16 or wider, within the bound.
No kernel may reach another device: no remote copies, remote signals or barrier semaphores. Data moves between devices by JAX's collectives and lax.ppermute only.
A program may use at most 128 MiB of HBM per device.

```python
import jax
import jax.numpy as jnp
from jax import lax

HEADS = 32
HEAD_DIM = 80
D = 2560
GROUPS = 4
SPAN = 8
TOK_DEV = 384
TOKENS = 12288
N_SEQ = 32


def draw_queries(key, part):
    key = jax.random.fold_in(key, 2)
    return jnp.clip(jax.random.normal(key, (TOKENS, D), jnp.float32), -6.0, 6.0).astype(jnp.bfloat16)


def draw_keys(key, part):
    key = jax.random.fold_in(key, 3)
    return jnp.clip(jax.random.normal(key, (TOKENS, D), jnp.float32), -6.0, 6.0).astype(jnp.bfloat16)


def draw_offsets(key, part):
    key = jax.random.fold_in(key, 9)
    per = HEADS // GROUPS
    orders = jnp.stack([jax.random.permutation(jax.random.fold_in(key, group), per) for group in range(GROUPS)], 0)
    rates = 2 ** jnp.arange(GROUPS, dtype=jnp.int32)
    return (orders % rates[:, None]).T.reshape(HEADS).astype(jnp.int32)


def block_scale(own_key, dims, cuts, least, high):
    def one(axis_at, shards_of):
        steps = jax.random.uniform(jax.random.fold_in(jax.random.fold_in(own_key, 6), axis_at), (shards_of,), jnp.float32, least / len(cuts), high / len(cuts))
        return jnp.repeat(jnp.exp(steps), dims[axis_at] // shards_of).reshape((-1,) + (1,) * (len(dims) - axis_at - 1))

    level = one(*cuts[0])
    for cut in cuts[1:]:
        level = level * one(*cut)
    return level


def scatter_about(rng, dims, scale, limit, cuts=(), kind=jnp.bfloat16):
    array = jax.random.normal(rng, dims, jnp.float32) * scale
    if len(cuts) > 0:
        array = block_scale(rng, dims, cuts, -0.22, 0.18) * array
    return jnp.clip(array, min=-limit, max=limit).astype(kind)


def setup_inputs(seed: int = 0) -> dict:
    seeds = jax.random.split(jax.random.key(seed), 7)
    return {
        "queries": draw_queries(jax.random.fold_in(seeds[6], 71), 0),
        "keys": draw_keys(jax.random.fold_in(seeds[6], 71), 0),
        "values": scatter_about(seeds[2], (TOKENS, D), 1.0, 6.0, ((0, 32), (1, 4))),
        "out_grad": scatter_about(seeds[3], (TOKENS, D), 1.0, 6.0, ((0, 32), (1, 4))),
        "out_weight": scatter_about(seeds[4], (D, D), D ** -0.5, 0.125, ((0, 4),)),
        "offsets": draw_offsets(jax.random.fold_in(seeds[6], 71), 0),
    }


NEG = -1e30


def pick_rows(x3, offs, rate):
    rows = x3.shape[0] // rate
    x4 = x3.reshape(rows, rate, x3.shape[1], x3.shape[2])
    chosen = jnp.arange(rate, dtype=jnp.int32)[:, None] == offs[None, :]
    return jnp.sum(jnp.where(chosen[None, :, :, None], x4, jnp.zeros((), x4.dtype)), axis=1).astype(x3.dtype)


def spread_rows(x3, offs, rate):
    rows = x3.shape[0]
    chosen = jnp.arange(rate, dtype=jnp.int32)[:, None] == offs[None, :]
    full = jnp.where(chosen[None, :, :, None], x3[:, None], jnp.zeros((), x3.dtype))
    return full.reshape(rows * rate, x3.shape[1], x3.shape[2])


def window_grads(query, key_rows, value_rows, grad_rows, segment):
    rows = query.shape[0]
    place = jnp.arange(rows, dtype=jnp.int32)
    visible = (segment[:, None] == segment[None, :]) & (place[None, :] <= place[:, None])
    scale = HEAD_DIM ** -0.5
    scores = jnp.dot(query, key_rows.T, preferred_element_type=jnp.float32) * scale
    masked = jnp.where(visible, scores, NEG)
    top = jnp.max(masked, axis=1, keepdims=True)
    expd = jnp.where(visible, jnp.exp(masked - top), 0.0)
    prob = expd / jnp.sum(expd, axis=1, keepdims=True)
    prob_b = prob.astype(jnp.bfloat16)
    attended = jnp.dot(prob_b, value_rows, preferred_element_type=jnp.float32)
    delta = jnp.sum(grad_rows.astype(jnp.float32) * attended, axis=1, keepdims=True)
    dprob = jnp.dot(grad_rows, value_rows.T, preferred_element_type=jnp.float32)
    dscore = (prob * (dprob - delta)).astype(jnp.bfloat16)
    query_part = (jnp.dot(dscore, key_rows, preferred_element_type=jnp.float32) * scale).astype(jnp.bfloat16)
    key_part = (jnp.dot(dscore.T, query, preferred_element_type=jnp.float32) * scale).astype(jnp.bfloat16)
    value_part = jnp.dot(prob_b.T, grad_rows, preferred_element_type=jnp.float32).astype(jnp.bfloat16)
    return query_part, key_part, value_part


def reference(queries, keys, values, out_grad, out_weight, offsets):
    attn_grad = jnp.dot(out_grad, out_weight.T, preferred_element_type=jnp.float32).astype(jnp.bfloat16)
    heads_per = HEADS // GROUPS
    windows = N_SEQ // SPAN
    offs_all = offsets.reshape(heads_per, GROUPS)
    grads = [[], [], []]
    for group in range(GROUPS):
        rate = 2 ** group
        rows = TOK_DEV // rate
        offs = offs_all[:, group]

        def prepare(whole):
            x3 = whole.reshape(TOKENS, heads_per, GROUPS, HEAD_DIM)[:, :, group, :]
            picked = pick_rows(x3, offs, rate)
            return picked.reshape(windows, SPAN * rows, heads_per, HEAD_DIM).transpose(2, 0, 1, 3)

        block_seg = jnp.arange(N_SEQ, dtype=jnp.int32) // rate
        segment = jnp.repeat(block_seg, rows).reshape(windows, SPAN * rows)

        def per_head(items):
            query_h, key_h, value_h, grad_h = items
            return lax.map(lambda w: window_grads(w[0], w[1], w[2], w[3], w[4]), (query_h, key_h, value_h, grad_h, segment))

        results = lax.map(per_head, (prepare(queries), prepare(keys), prepare(values), prepare(attn_grad)))
        for slot in range(3):
            back = results[slot].transpose(1, 2, 0, 3).reshape(TOKENS // rate, heads_per, HEAD_DIM)
            grads[slot].append(spread_rows(back, offs, rate))
    query_grad = jnp.stack(grads[0], 2).reshape(TOKENS, HEADS * HEAD_DIM)
    key_grad = jnp.stack(grads[1], 2).reshape(TOKENS, HEADS * HEAD_DIM)
    value_grad = jnp.stack(grads[2], 2).reshape(TOKENS, HEADS * HEAD_DIM)
    return (query_grad, key_grad, value_grad)
```

```python
import functools

import jax
import jax.numpy as jnp
from jax import lax
from jax.experimental import pallas as pl
from jax.experimental.pallas import tpu as pltpu
from jax.sharding import PartitionSpec as P

HEAD_DIM = 80
GROUPS = 4
SLOT = 128
PAIR = 2 * SLOT
NEG = -1e30
PLACE = 4
SCALE = HEAD_DIM ** (-0.5)
LOG2E = 1.4426950408889634
ORDER = {1: (0, 1), 2: (0, 1, 2, 3), 3: (0, 1, 2, 3, 4, 6, 5, 7)}
NT = (((1,), (1,)), ((), ()))
NN = (((1,), (0,)), ((), ()))
TN = (((0,), (0,)), ((), ()))
F32 = jnp.float32
BF16 = jnp.bfloat16


def dot(a, b, dims):
    return lax.dot_general(a, b, dims, preferred_element_type=F32)


def iota(shape, axis):
    return lax.broadcasted_iota(jnp.int32, shape, axis)


def window(head):
    low = HEAD_DIM * head
    start = low // SLOT * SLOT
    width = SLOT if low - start + HEAD_DIM <= SLOT else 2 * SLOT
    return start, width, low - start


def to_slot(x, shift, ones=0):
    if shift:
        x = pltpu.roll(x, x.shape[1] - shift, 1)
    x = x[:, :SLOT]
    lane = iota(x.shape, 1)
    fill = jnp.where(lane < HEAD_DIM + ones, 1.0, 0.0) if ones else 0.0
    return jnp.where(lane < HEAD_DIM, x, fill)


def pick(offset, rows, rate, tok):
    return (iota((rows, tok), 1) == iota((rows, tok), 0) * rate + offset).astype(BF16)


def starts_of(tok):
    rows = [tok >> g for g in range(GROUPS)]
    first = {g: sum(rows[1:g]) for g in range(1, GROUPS)}
    return rows, first


def select_kernel(
    info,
    offs_hbm,
    q_hbm,
    k_hbm,
    v_hbm,
    og_hbm,
    w_hbm,
    s0_ref,
    sall_ref,
    s23_ref,
    pick_scr,
    spread_ref,
    own_ref,
    wt_ref,
    x_scr,
    offs,
    sems,
):
    tok = x_scr.shape[1]
    width = x_scr.shape[2]
    rows, first = starts_of(tok)
    copies = [
        pltpu.make_async_copy(ref, x_scr.at[i], sems.at[i])
        for i, ref in enumerate((q_hbm, k_hbm, v_hbm))
    ]
    scalars = pltpu.make_async_copy(offs_hbm, offs, sems.at[3])
    copies.append(pltpu.make_async_copy(og_hbm, own_ref, sems.at[4]))
    for i in range(4):
        column = pl.ds(pl.multiple_of(info[i] * width, SLOT), width)
        copies.append(pltpu.make_async_copy(w_hbm.at[:, column], wt_ref.at[i], sems.at[5 + i]))
    scalars.start()
    for copy in copies:
        copy.start()
    scalars.wait()
    for a in range(2):
        spread_ref[a] = spread_matrix(offs, a, (1, 2, 3), tok)
        for g in range(1, GROUPS):
            chosen = pick(offs[GROUPS * a + g], rows[g], 1 << g, tok)
            pick_scr[a, first[g] : first[g] + rows[g], :] = chosen
    for i in range(3):
        copies[i].wait()
        for a in range(2):
            col = (2 * i + a) * SLOT
            for g in range(GROUPS):
                start, width, shift = window(GROUPS * a + g)
                x = x_scr[i, :, start : start + width]
                if g == 0:
                    y = to_slot(x.astype(F32), shift, 2 if i == 2 else 0)
                    s0_ref[:, col : col + SLOT] = y.astype(BF16)
                    continue
                at = first[g]
                x = dot(pick_scr[a, at : at + rows[g], :], x, NN)
                y = to_slot(x, shift, 2 if i == 2 else 0).astype(BF16)
                sall_ref[at : at + rows[g], col : col + SLOT] = y
                if g > 1:
                    at -= rows[1]
                    s23_ref[at : at + rows[g], col : col + SLOT] = y
    for copy in copies[3:]:
        copy.wait()


def forward_block(q, k, mask):
    st = jnp.where(mask, dot(k, q, NT), NEG)
    top = jnp.max(st, axis=0, keepdims=True)
    e = jnp.exp2((st - top) * (SCALE * LOG2E))
    total = jnp.sum(e, axis=0, keepdims=True)
    return e * (1.0 / total)


def own_forward_kernel(s0_ref, p_ref, o_ref):
    tok = s0_ref.shape[0]
    for b in range(tok // SLOT):
        lo, hi = b * SLOT, (b + 1) * SLOT
        mask = iota((hi, SLOT), 0) <= iota((hi, SLOT), 1) + lo
        for a in range(2):
            at = a * SLOT
            q = s0_ref[lo:hi, at : at + SLOT]
            k = s0_ref[:hi, PAIR + at : PAIR + at + SLOT]
            v = s0_ref[:hi, 2 * PAIR + at : 2 * PAIR + at + SLOT]
            p = forward_block(q, k, mask).astype(BF16)
            p_ref[a, :hi, lo:hi] = p
            if hi < tok:
                p_ref[a, hi:, lo:hi] = jnp.zeros((tok - hi, SLOT), BF16)
            o_ref[lo:hi, at : at + SLOT] = dot(p, v, TN)


def assemble(g, tok, own, near, r2, r4, r6, d, d2):
    rows, first = starts_of(tok)
    n = rows[g]
    at = first[g]
    low = at - rows[1]
    d4 = d2 + r2.shape[0]
    parts = [(own, at), (near, at)]
    if g > 1:
        parts += [(r2, low), (d, d2 + low)]
    if g > 2:
        parts += [(r4, 0), (r6, 0), (d, d4), (d, d4 + n)]
    return n, parts


def places(g, n, place, shape, axis):
    s = iota(shape, axis)
    code = jnp.zeros(shape, jnp.int32)
    back = jnp.zeros(shape, jnp.int32)
    for i, m in enumerate(ORDER[g]):
        if i:
            code = jnp.where(s >= i * n, m, code)
            back = jnp.where(s >= i * n, i * n, back)
    return (code ^ place) * n + s - back


def segment_forward_kernel(
    info, own, r2, r4, r6, d, f_ref, o1_ref, o23_ref, q1, q2, q3, k1, k2, k3
):
    tok = f_ref.shape[1]
    rows, first = starts_of(tok)
    for g, pq, pk in ((1, q1, k1), (2, q2, k2), (3, q3, k3)):
        n, parts = assemble(g, tok, own, d, r2, r4, r6, d, own.shape[0])
        for i, (ref, at) in enumerate(parts):
            f_ref[g - 1, i * n : (i + 1) * n, :] = ref[at : at + n, :]
        place = lax.rem(info[PLACE], 1 << g)
        at_key = places(g, n, place, (tok, SLOT), 0)
        at_query = places(g, n, place, (1, tok), 1)
        for b in range(tok // SLOT):
            lo, hi = b * SLOT, (b + 1) * SLOT
            mask = at_key <= at_query[:, lo:hi]
            for a in range(2):
                c = a * SLOT
                q = f_ref[g - 1, lo:hi, c : c + SLOT]
                k = f_ref[g - 1, :, PAIR + c : PAIR + c + SLOT]
                p = forward_block(q, k, mask)
                pk[a, :, lo:hi] = p[:n].astype(BF16)
                own_rows = min(n, hi) - lo
                if own_rows > 0:
                    mine = jnp.transpose(p)[:own_rows].astype(BF16)
                    pq[a, lo : lo + own_rows, :] = mine
                    v = f_ref[g - 1, :, 2 * PAIR + c : 2 * PAIR + c + SLOT]
                    o = dot(mine, v, NN)
                    if g == 1:
                        o1_ref[lo : lo + own_rows, c : c + SLOT] = o
                    else:
                        at = first[g] - rows[1] + lo
                        o23_ref[at : at + own_rows, c : c + SLOT] = o


def project_own_kernel(own, wt, acc):
    for b in range(4):
        lo = 2 * HEAD_DIM * b
        acc[b] = dot(own[...], wt[0, lo : lo + 2 * HEAD_DIM], NT)


def project_near_kernel(acc_in, left, right, wt, acc):
    for b in range(4):
        lo = 2 * HEAD_DIM * b
        acc[b] = (
            acc_in[b]
            + dot(left[...], wt[1, lo : lo + 2 * HEAD_DIM], NT)
            + dot(right[...], wt[2, lo : lo + 2 * HEAD_DIM], NT)
        )


def with_delta(g, o):
    delta = jnp.sum(g.astype(BF16).astype(F32) * o, axis=1, keepdims=True)
    high = delta.astype(BF16).astype(F32)
    lane = iota(g.shape, 1)
    g = jnp.where(lane == HEAD_DIM, -high, g)
    return jnp.where(lane == HEAD_DIM + 1, high - delta, g).astype(BF16)


def finish_pairs(b0, acc, far1, far2, wt, x_scr, g_scr):
    half = far1.shape[0]
    x_scr[:half] = far1[...]
    x_scr[half:] = far2[...]
    wide = 2 * HEAD_DIM
    parts = []
    for a in range(2):
        b = 2 * a + b0
        lo = wide * b
        parts.append(acc[b] + dot(x_scr[...], wt[3, lo : lo + wide], NT))
        g_scr[a, :, wide:] = jnp.zeros((2 * half, PAIR - wide), BF16)
    for a in range(2):
        g_scr[a, :, :wide] = parts[a].astype(BF16)


def finish_low_kernel(picks, acc, far1, far2, wt, o23, g23_ref, x_scr, g_scr):
    tok = x_scr.shape[0]
    rows, first = starts_of(tok)
    finish_pairs(1, acc, far1, far2, wt, x_scr, g_scr)
    for g in (2, 3):
        for a in range(2):
            c = a * SLOT
            at = first[g] - rows[1]
            n = rows[g]
            x = dot(picks[a, first[g] : first[g] + n, :], g_scr[a], NN)
            x = to_slot(x, HEAD_DIM * (g - 2))
            g23_ref[at : at + n, c : c + SLOT] = with_delta(x, o23[at : at + n, c : c + SLOT])


def finish_high_kernel(picks, acc, far1, far2, wt, o0, o1, g23, g0_ref, gall_ref, x_scr, g_scr):
    tok = x_scr.shape[0]
    n = tok // 2
    finish_pairs(0, acc, far1, far2, wt, x_scr, g_scr)
    gall_ref[n:, :] = g23[...]
    for a in range(2):
        c = a * SLOT
        x = to_slot(g_scr[a, :, :SLOT].astype(F32), 0)
        g0_ref[:, c : c + SLOT] = with_delta(x, o0[:, c : c + SLOT])
        x = to_slot(dot(picks[a, :n, :], g_scr[a], NN), HEAD_DIM)
        gall_ref[:n, c : c + SLOT] = with_delta(x, o1[:, c : c + SLOT])


def own_backward_kernel(s0_ref, p_ref, g_ref, d_ref, ds_scr):
    tok = s0_ref.shape[0]
    for b in range(tok // SLOT):
        lo, hi = b * SLOT, (b + 1) * SLOT
        for a in range(2):
            at = a * SLOT
            v = s0_ref[:hi, 2 * PAIR + at : 2 * PAIR + at + SLOT]
            x = dot(v, g_ref[lo:hi, at : at + SLOT], NT)
            ds_scr[a, :hi, lo:hi] = (p_ref[a, :hi, lo:hi].astype(F32) * x).astype(BF16)
            if hi < tok:
                ds_scr[a, hi:, lo:hi] = jnp.zeros((tok - hi, SLOT), BF16)
    for a in range(2):
        at = a * SLOT
        q = s0_ref[:, at : at + SLOT]
        k = s0_ref[:, PAIR + at : PAIR + at + SLOT]
        ds = ds_scr[a]
        dq = dot(ds, k, TN) * SCALE
        dk = dot(ds, q, NN) * SCALE
        dv = clear(dot(p_ref[a], g_ref[:, at : at + SLOT], NN))
        d_ref[:, at : at + SLOT] = dq.astype(BF16)
        d_ref[:, PAIR + at : PAIR + at + SLOT] = dk.astype(BF16)
        d_ref[:, 2 * PAIR + at : 2 * PAIR + at + SLOT] = dv.astype(BF16)


def clear(x):
    return jnp.where(iota(x.shape, 1) < HEAD_DIM, x, 0.0)


def shifted_lanes(x, by):
    slot, by = by // SLOT, by % SLOT
    if by == 0:
        return slot, x
    if by + HEAD_DIM <= SLOT:
        return slot, pltpu.roll(x, by, 1)
    return slot, pltpu.roll(jnp.concatenate([x, jnp.zeros_like(x)], 1), by, 1)


def spread_matrix(offs, a, groups, tok):
    rows, _ = starts_of(tok)
    width = sum(rows[g] for g in groups)
    col = iota((1, width), 1)
    at = 0
    target = jnp.zeros((1, width), jnp.int32)
    for g in groups:
        here = (col - at) * (1 << g) + offs[GROUPS * a + g]
        target = jnp.where(col >= at, here, target) if at else here
        at += rows[g]
    return (iota((tok, width), 0) == target).astype(BF16)


def place_rows(b_scr, at, g, a, x):
    n = x.shape[0]
    slot, y = shifted_lanes(x, HEAD_DIM * g + a * (GROUPS * HEAD_DIM % SLOT))
    wide = y.shape[1] // SLOT
    zero = jnp.zeros((n, SLOT), BF16)
    for s in range(3):
        if slot <= s < slot + wide:
            part = y[:, (s - slot) * SLOT : (s - slot + 1) * SLOT].astype(BF16)
        else:
            part = zero
        b_scr[at : at + n, s * SLOT : (s + 1) * SLOT] = part


def store_halves(out_ref, halves, base=None):
    lo, hi = halves
    width = out_ref.shape[1]
    tiles = [lo[:, :SLOT], lo[:, SLOT:PAIR], lo[:, PAIR:] + hi[:, :SLOT]]
    tiles += [hi[:, SLOT:PAIR], hi[:, PAIR:]]
    for i, tile in enumerate(tiles):
        if base is not None:
            tile = tile + base[:, i * SLOT : (i + 1) * SLOT].astype(F32)
        out_ref[:, i * SLOT : (i + 1) * SLOT] = tile.astype(BF16)


def add_own(full, a, x):
    slot, y = shifted_lanes(x.astype(F32), a * (GROUPS * HEAD_DIM % SLOT))
    wide = y.shape[1]
    return jnp.concatenate([full[:, :wide] + y, full[:, wide:]], 1)


def query_kernel(spreads, d_ref, f_ref, gall_ref, q1, q2, q3, out_ref, b_scr):
    tok = out_ref.shape[0]
    rows, first = starts_of(tok)
    chain = [(g, a) for g in (1, 2, 3) for a in range(2)]
    pqs = {1: q1, 2: q2, 3: q3}
    grads = {}
    for g, a in chain:
        c = a * SLOT
        v = f_ref[g - 1, :, 2 * PAIR + c : 2 * PAIR + c + SLOT]
        x = dot(gall_ref[first[g] : first[g] + rows[g], c : c + SLOT], v, NT)
        grads[g, a] = (pqs[g][a].astype(F32) * x).astype(BF16)
    for g, a in chain:
        k = f_ref[g - 1, :, PAIR + a * SLOT : PAIR + (a + 1) * SLOT]
        place_rows(b_scr.at[a], first[g], g, a, dot(grads[g, a], k, NN) * SCALE)
    halves = []
    for a in range(2):
        full = dot(spreads[a], b_scr[a], NN)
        halves.append(add_own(full, a, d_ref[:, a * SLOT : (a + 1) * SLOT]))
    store_halves(out_ref, halves)


def key_value_high_kernel(spreads, d_ref, f_ref, own, near, pk, key_ref, value_ref, g_scr, b_scr):
    tok = key_ref.shape[0]
    n = tok // 2
    g_scr[:n] = own[:n]
    g_scr[n:] = near[:n]
    key_value_rows((1,), tok, f_ref, (g_scr,), {1: pk}, b_scr)
    for i, out_ref in enumerate((key_ref, value_ref)):
        parts = []
        for a in range(2):
            c = (i + 1) * PAIR + a * SLOT
            x = dot(spreads[a, :, :n], b_scr[i, a], NN)
            parts.append(add_own(x, a, d_ref[:, c : c + SLOT]))
        store_halves(out_ref, parts)


def key_value_rows(groups, tok, f_ref, g_scr, pks, b_scr):
    rows, first = starts_of(tok)
    chain = [(g, a) for g in groups for a in range(2)]
    grads = {}
    for g, a in chain:
        c = a * SLOT
        v = f_ref[g - 1, : rows[g], 2 * PAIR + c : 2 * PAIR + c + SLOT]
        x = dot(v, g_scr[g - groups[0]][:, c : c + SLOT], NT)
        grads[g, a] = (pks[g][a].astype(F32) * x).astype(BF16)
    for g, a in chain:
        q = f_ref[g - 1, :, a * SLOT : (a + 1) * SLOT]
        at = first[g] - first[groups[0]]
        place_rows(b_scr.at[0, a], at, g, a, dot(grads[g, a], q, NN) * SCALE)
    for g, a in chain:
        gg = g_scr[g - groups[0]][:, a * SLOT : (a + 1) * SLOT]
        at = first[g] - first[groups[0]]
        place_rows(b_scr.at[1, a], at, g, a, clear(dot(pks[g][a], gg, NN)))


def key_value_low_kernel(
    spreads,
    query_in,
    key_in,
    value_in,
    f_ref,
    own,
    near,
    r2,
    r4,
    r6,
    d,
    k2,
    k3,
    query_out,
    key_out,
    value_out,
    g_scr,
    b_scr,
    key_scr,
    value_scr,
    sems,
):
    tok = key_scr.shape[0]
    n = tok // 2
    copies = [
        pltpu.make_async_copy(x, out, sems.at[i])
        for i, (x, out) in enumerate(
            ((query_in, query_out), (key_scr, key_out), (value_scr, value_out))
        )
    ]
    copies[0].start()
    for g in (2, 3):
        m, parts = assemble(g, tok, own, near, r2, r4, r6, d, 0)
        for i, (ref, at) in enumerate(parts):
            g_scr[g - 2, i * m : (i + 1) * m, :] = ref[at : at + m, :]
    key_value_rows((2, 3), tok, f_ref, (g_scr.at[0], g_scr.at[1]), {2: k2, 3: k3}, b_scr)
    for i, (base, out) in enumerate(((key_in, key_scr), (value_in, value_scr))):
        parts = [dot(spreads[a, :, n:], b_scr[i, a], NN) for a in range(2)]
        store_halves(out, parts, base)
        copies[i + 1].start()
    for copy in copies:
        copy.wait()


VM = pl.BlockSpec(memory_space=pltpu.VMEM)
SM = pl.BlockSpec(memory_space=pltpu.SMEM)
HB = pl.BlockSpec(memory_space=pltpu.HBM)


def shape(*dims, dtype=BF16):
    return jax.ShapeDtypeStruct(dims, dtype)


def scratch(*dims, dtype=BF16):
    return pltpu.VMEM(dims, dtype)


def call(kernel, outs, operands, specs="", scratches=(), name=None, out=VM):
    kinds = {"s": SM, "h": HB, "v": VM}
    operands = [
        pltpu.with_memory_space_constraint(x, pltpu.HBM) if kind == "h" else x
        for x, kind in zip(operands, specs + "v" * len(operands))
    ]
    specs = [kinds[x] for x in specs]
    specs += [VM] * (len(operands) - len(specs))
    return pl.pallas_call(
        kernel,
        out_shape=outs,
        in_specs=specs,
        out_specs=jax.tree.map(lambda _: out, outs),
        scratch_shapes=list(scratches),
        compiler_params=pltpu.CompilerParams(vmem_limit_bytes=20 << 20),
        cost_estimate=pl.CostEstimate(
            flops=0, bytes_accessed=0, transcendentals=0
        ),
        name=name,
    )(*operands)


def on_device(queries, keys, values, out_grad, out_weight, offsets):
    tok, width = queries.shape
    rows, first = starts_of(tok)
    half = tok // 2
    index = lax.axis_index("seq")
    column = lax.axis_index("head")
    n_head = lax.axis_size("head")
    n_seq = lax.axis_size("seq")
    right_way = [(i, (i + 1) % n_head) for i in range(n_head)]
    left_way = [(i, (i - 1) % n_head) for i in range(n_head)]
    dma = pltpu.SemaphoreType.DMA

    def swap(x, mask):
        return lax.ppermute(x, "seq", [(i, i ^ mask) for i in range(n_seq)])

    def after(x, *others):
        return lax.optimization_barrier((x,) + others)[0]

    wide = 2 * HEAD_DIM
    n_all = sum(rows[1:])
    n_low = n_all - rows[1]

    left = lax.ppermute(out_grad, "head", right_way)
    right = lax.ppermute(out_grad, "head", left_way)

    blocks = [column, (column + n_head - 1) % n_head, (column + 1) % n_head]
    blocks += [(column + 2) % n_head, index]
    info = jnp.stack(blocks).astype(jnp.int32)

    s0, sall, s23, picks, spreads, own, wt = call(
        select_kernel,
        (
            shape(tok, 3 * PAIR),
            shape(n_all, 3 * PAIR),
            shape(n_low, 3 * PAIR),
            shape(2, n_all, tok),
            shape(2, tok, n_all),
            shape(tok, width),
            shape(4, width, width),
        ),
        (info, offsets, queries, keys, values, out_grad, out_weight),
        specs="shhhhhh",
        scratches=(scratch(3, tok, width), pltpu.SMEM((2 * GROUPS,), jnp.int32), dma((9,))),
        name="select",
    )

    def far_swaps(low):
        last = low[rows[2] :]
        r4 = swap(last, 4)
        r2 = swap(low, 2)
        return r2, r4, swap(last, 6)

    r2, r4, r6 = far_swaps(s23)
    acc_own = call(
        project_own_kernel,
        shape(4, tok, wide, dtype=F32),
        (own, wt),
        name="project_own",
    )
    p0, o0 = call(
        own_forward_kernel,
        (shape(2, tok, tok), shape(tok, PAIR, dtype=F32)),
        (s0,),
        name="own_forward",
    )
    left, right, acc_own, o0 = lax.optimization_barrier((left, right, acc_own, o0))
    far1 = lax.ppermute(left[:half], "head", right_way)
    far2 = lax.ppermute(right[half:], "head", left_way)
    r2, r4, r6, o0 = lax.optimization_barrier((r2, r4, r6, o0))
    d = swap(jnp.concatenate([sall, r2, r4, r6], 0), 1)
    acc = call(
        project_near_kernel,
        shape(4, tok, wide, dtype=F32),
        (after(acc_own, r2), left, right, wt),
        name="project_near",
    )
    d = after(d, acc)
    seg = call(
        segment_forward_kernel,
        (shape(3, tok, 3 * PAIR), shape(rows[1], PAIR, dtype=F32), shape(n_low, PAIR, dtype=F32))
        + tuple(shape(2, rows[g], tok) for g in (1, 2, 3)) * 2,
        (info, sall, r2, r4, r6, d),
        specs="s",
        name="segment_forward",
    )
    full, o1, o23 = seg[:3]
    pq, pk = seg[3:6], seg[6:9]

    pair_scratch = (scratch(tok, width), scratch(2, tok, PAIR))
    g23 = call(
        finish_low_kernel,
        shape(n_low, PAIR),
        (picks, acc, far1, far2, wt, o23),
        scratches=pair_scratch,
        name="finish_low",
    )
    g_far = far_swaps(g23)
    g0, gall = call(
        finish_high_kernel,
        (shape(tok, PAIR), shape(n_all, PAIR)),
        (picks, acc, far1, far2, wt, o0, o1, g23),
        scratches=pair_scratch,
        name="finish_high",
    )
    g_near = swap(gall, 1)
    d0 = call(
        own_backward_kernel,
        shape(tok, 3 * PAIR),
        (s0, p0, g0),
        scratches=(scratch(2, tok, tok),),
        name="own_backward",
    )
    key_part, value_part = call(
        key_value_high_kernel,
        (shape(tok, width), shape(tok, width)),
        (spreads, d0, full, gall, g_near, pk[0]),
        scratches=(scratch(tok, PAIR), scratch(2, 2, rows[1], 3 * SLOT)),
        name="key_value_high",
    )
    g_far = lax.optimization_barrier(g_far + (key_part,))[:3]
    g_d = swap(jnp.concatenate(g_far, 0), 1)
    query_part = call(
        query_kernel,
        shape(tok, width),
        (spreads, after(d0, g_far[1]), full, gall) + tuple(pq),
        scratches=(scratch(2, n_all, 3 * SLOT),),
        name="query_side",
    )
    return tuple(
        call(
            key_value_low_kernel,
            (shape(tok, width),) * 3,
            (spreads, query_part, key_part, value_part, full, gall, g_near)
            + g_far
            + (g_d,)
            + tuple(pk[1:]),
            scratches=(
                scratch(2, tok, PAIR),
                scratch(2, 2, n_low, 3 * SLOT),
                scratch(tok, width),
                scratch(tok, width),
                dma((3,)),
            ),
            name="key_value_low",
            out=HB,
        )
    )


def solution(mesh):
    placed = (
        P("seq", "head"),
        P("seq", "head"),
        P("seq", "head"),
        P("seq", "head"),
        P("head", None),
        P("head"),
    )
    return jax.shard_map(
        on_device,
        mesh=mesh,
        in_specs=placed,
        out_specs=(P("seq", "head"), P("seq", "head"), P("seq", "head")),
        check_vma=False,
    )
```

```python
import functools

import jax
import jax.numpy as jnp
from jax import lax
from jax.experimental import pallas as pl
from jax.experimental.pallas import tpu as pltpu
from jax.sharding import PartitionSpec as P

HEAD_DIM = 80
GROUPS = 4
SLOT = 128
PAIR = 2 * SLOT
SPARE = SLOT - HEAD_DIM
NEG = -1e30
PLACE = 4
SCALE = HEAD_DIM ** (-0.5)
LOG2E = 1.4426950408889634
ORDER = {1: (0, 1), 2: (0, 1, 2, 3), 3: (0, 1, 2, 3, 4, 6, 5, 7)}
NT = (((1,), (1,)), ((), ()))
NN = (((1,), (0,)), ((), ()))
TN = (((0,), (0,)), ((), ()))
F32 = jnp.float32
BF16 = jnp.bfloat16


def dot(a, b, dims):
    return lax.dot_general(a, b, dims, preferred_element_type=F32)


def iota(shape, axis):
    return lax.broadcasted_iota(jnp.int32, shape, axis)


def window(head):
    low = HEAD_DIM * head
    start = low // SLOT * SLOT
    width = SLOT if low - start + HEAD_DIM <= SLOT else 2 * SLOT
    return start, width, low - start


def to_slot(x, shift, ones=0):
    if shift:
        x = pltpu.roll(x, x.shape[1] - shift, 1)
    x = x[:, :SLOT]
    lane = iota(x.shape, 1)
    fill = jnp.where(lane < HEAD_DIM + ones, 1.0, 0.0) if ones else 0.0
    return jnp.where(lane < HEAD_DIM, x, fill)


def pick(offset, rows, rate, tok):
    return (iota((rows, tok), 1) == iota((rows, tok), 0) * rate + offset).astype(BF16)


def starts_of(tok):
    rows = [tok >> g for g in range(GROUPS)]
    first = {g: sum(rows[1:g]) for g in range(1, GROUPS)}
    return rows, first


def select_kernel(
    info,
    offs_hbm,
    q_hbm,
    k_hbm,
    v_hbm,
    og_hbm,
    w_hbm,
    s0_ref,
    sall_ref,
    s23_ref,
    pick_scr,
    spread_ref,
    own_ref,
    wt_ref,
    x_scr,
    offs,
    sems,
):
    tok = x_scr.shape[1]
    width = x_scr.shape[2]
    rows, first = starts_of(tok)
    copies = [
        pltpu.make_async_copy(ref, x_scr.at[i], sems.at[i])
        for i, ref in enumerate((q_hbm, k_hbm, v_hbm))
    ]
    scalars = pltpu.make_async_copy(offs_hbm, offs, sems.at[3])
    copies.append(pltpu.make_async_copy(og_hbm, own_ref, sems.at[4]))
    for i in range(4):
        column = pl.ds(pl.multiple_of(info[i] * width, SLOT), width)
        copies.append(pltpu.make_async_copy(w_hbm.at[:, column], wt_ref.at[i], sems.at[5 + i]))
    scalars.start()
    for copy in copies:
        copy.start()
    scalars.wait()
    for a in range(2):
        spread_ref[a] = spread_matrix(offs, a, (1, 2, 3), tok)
        for g in range(1, GROUPS):
            chosen = pick(offs[GROUPS * a + g], rows[g], 1 << g, tok)
            pick_scr[a, first[g] : first[g] + rows[g], :] = chosen
    for i in range(3):
        copies[i].wait()
        for a in range(2):
            for g in range(GROUPS):
                start, width, shift = window(GROUPS * a + g)
                x = x_scr[i, :, start : start + width]
                if g == 0:
                    col = (2 * i + a) * SLOT
                    y = to_slot(x.astype(F32), shift, 2 if i == 2 else 0)
                    s0_ref[:, col : col + SLOT] = y.astype(BF16)
                    continue
                at, n = first[g], rows[g]
                y = to_slot(dot(pick_scr[a, at : at + n, :], x, NN), shift)
                if i < 2:
                    col = (2 * i + a) * SLOT
                    sall_ref[at : at + n, col : col + SLOT] = y.astype(BF16)
                    continue
                for half, by in ((0, HEAD_DIM), (1, HEAD_DIM - SPARE)):
                    col = (2 * a + half) * SLOT
                    spare = pltpu.roll(y, by, 1).astype(BF16)
                    lane = iota((n, SLOT), 1)
                    y_old = sall_ref[at : at + n, col : col + SLOT]
                    sall_ref[at : at + n, col : col + SLOT] = jnp.where(
                        lane < HEAD_DIM, y_old, spare
                    )
    s23_ref[...] = sall_ref[rows[1] :, :]
    for copy in copies[3:]:
        copy.wait()


def forward_block(q, k, mask):
    st = jnp.where(mask, dot(k, q, NT), NEG)
    top = jnp.max(st, axis=0, keepdims=True)
    e = jnp.exp2((st - top) * (SCALE * LOG2E))
    total = jnp.sum(e, axis=0, keepdims=True)
    return e * (1.0 / total)


def own_forward_kernel(s0_ref, p_ref, o_ref):
    tok = s0_ref.shape[0]
    for b in range(tok // SLOT):
        lo, hi = b * SLOT, (b + 1) * SLOT
        mask = iota((hi, SLOT), 0) <= iota((hi, SLOT), 1) + lo
        for a in range(2):
            at = a * SLOT
            q = s0_ref[lo:hi, at : at + SLOT]
            k = s0_ref[:hi, PAIR + at : PAIR + at + SLOT]
            v = s0_ref[:hi, 2 * PAIR + at : 2 * PAIR + at + SLOT]
            p = forward_block(q, k, mask).astype(BF16)
            p_ref[a, :hi, lo:hi] = p
            if hi < tok:
                p_ref[a, hi:, lo:hi] = jnp.zeros((tok - hi, SLOT), BF16)
            o_ref[lo:hi, at : at + SLOT] = dot(p, v, TN)


def parts_of(g, tok, own, near, r2, d2, r4, r6, d4, d6):
    rows, first = starts_of(tok)
    low = first[g] - rows[1]

    def at(source):
        return source[0], source[1] + low

    parts = [at(own), at(near), at(r2), at(d2)]
    return parts + [r4, r6, d4, d6] if g > 2 else parts


def unpack(out, at, x):
    n = x.shape[0]
    lane = iota((n, SLOT), 1)
    tiles = [x[:, i * SLOT : (i + 1) * SLOT].astype(F32) for i in range(4)]
    slots = [jnp.where(lane < HEAD_DIM, t, 0.0) for t in tiles]
    ones = jnp.where(lane < HEAD_DIM + 2, 1.0, 0.0)
    for a in range(2):
        low = pltpu.roll(tiles[2 * a], SPARE, 1)
        high = pltpu.roll(tiles[2 * a + 1], SLOT - HEAD_DIM + SPARE, 1)
        slots.append(jnp.where(lane < SPARE, low, jnp.where(lane < HEAD_DIM, high, ones)))
    for i, slot in enumerate(slots):
        out[at : at + n, i * SLOT : (i + 1) * SLOT] = slot.astype(BF16)


def places(g, n, place, shape, axis):
    s = iota(shape, axis)
    code = jnp.zeros(shape, jnp.int32)
    back = jnp.zeros(shape, jnp.int32)
    for i, m in enumerate(ORDER[g]):
        if i:
            code = jnp.where(s >= i * n, m, code)
            back = jnp.where(s >= i * n, i * n, back)
    return (code ^ place) * n + s - back


def segment_forward_kernel(
    info, own, near1, da, r2, r4, r6, db, f_ref, o1_ref, o23_ref, q1, q2, q3, k1, k2, k3
):
    tok = f_ref.shape[1]
    rows, first = starts_of(tok)
    for g, pq, pk in ((1, q1, k1), (2, q2, k2), (3, q3, k3)):
        n, low = rows[g], r2.shape[0]
        parts = [(own, 0), (near1, 0)]
        if g > 1:
            parts = parts_of(
                g, tok, (own, rows[1]), (da, 0), (r2, 0), (db, 0), (r4, 0), (r6, 0), (db, low), (da, low)
            )
        for i, (ref, at) in enumerate(parts):
            unpack(f_ref.at[g - 1], i * n, ref[at : at + n, :])
        place = lax.rem(info[PLACE], 1 << g)
        at_key = places(g, n, place, (tok, SLOT), 0)
        at_query = places(g, n, place, (1, tok), 1)
        for b in range(tok // SLOT):
            lo, hi = b * SLOT, (b + 1) * SLOT
            mask = at_key <= at_query[:, lo:hi]
            for a in range(2):
                c = a * SLOT
                q = f_ref[g - 1, lo:hi, c : c + SLOT]
                k = f_ref[g - 1, :, PAIR + c : PAIR + c + SLOT]
                p = forward_block(q, k, mask)
                pk[a, :, lo:hi] = p[:n].astype(BF16)
                own_rows = min(n, hi) - lo
                if own_rows > 0:
                    mine = jnp.transpose(p)[:own_rows].astype(BF16)
                    pq[a, lo : lo + own_rows, :] = mine
                    v = f_ref[g - 1, :, 2 * PAIR + c : 2 * PAIR + c + SLOT]
                    o = dot(mine, v, NN)
                    if g == 1:
                        o1_ref[lo : lo + own_rows, c : c + SLOT] = o
                    else:
                        at = first[g] - rows[1] + lo
                        o23_ref[at : at + own_rows, c : c + SLOT] = o


def project_own_kernel(own, wt, acc):
    for b in range(4):
        lo = 2 * HEAD_DIM * b
        acc[b] = dot(own[...], wt[0, lo : lo + 2 * HEAD_DIM], NT)


def project_near_kernel(acc_in, left, right, wt, acc):
    for b in range(4):
        lo = 2 * HEAD_DIM * b
        acc[b] = (
            acc_in[b]
            + dot(left[...], wt[1, lo : lo + 2 * HEAD_DIM], NT)
            + dot(right[...], wt[2, lo : lo + 2 * HEAD_DIM], NT)
        )


def with_delta(g, o):
    delta = jnp.sum(g.astype(BF16).astype(F32) * o, axis=1, keepdims=True)
    high = delta.astype(BF16).astype(F32)
    lane = iota(g.shape, 1)
    g = jnp.where(lane == HEAD_DIM, -high, g)
    return jnp.where(lane == HEAD_DIM + 1, high - delta, g).astype(BF16)


def finish_pairs(b0, acc, far1, far2, wt, x_scr, g_scr):
    half = far1.shape[0]
    x_scr[:half] = far1[...]
    x_scr[half:] = far2[...]
    wide = 2 * HEAD_DIM
    parts = []
    for a in range(2):
        b = 2 * a + b0
        lo = wide * b
        parts.append(acc[b] + dot(x_scr[...], wt[3, lo : lo + wide], NT))
        g_scr[a, :, wide:] = jnp.zeros((2 * half, PAIR - wide), BF16)
    for a in range(2):
        g_scr[a, :, :wide] = parts[a].astype(BF16)


def finish_low_kernel(picks, acc, far1, far2, wt, o23, g23_ref, x_scr, g_scr):
    tok = x_scr.shape[0]
    rows, first = starts_of(tok)
    finish_pairs(1, acc, far1, far2, wt, x_scr, g_scr)
    for g in (2, 3):
        for a in range(2):
            c = a * SLOT
            at = first[g] - rows[1]
            n = rows[g]
            x = dot(picks[a, first[g] : first[g] + n, :], g_scr[a], NN)
            x = to_slot(x, HEAD_DIM * (g - 2))
            g23_ref[at : at + n, c : c + SLOT] = with_delta(x, o23[at : at + n, c : c + SLOT])


def finish_high_kernel(picks, acc, far1, far2, wt, o0, o1, g0_ref, g1_ref, x_scr, g_scr):
    tok = x_scr.shape[0]
    n = tok // 2
    finish_pairs(0, acc, far1, far2, wt, x_scr, g_scr)
    for a in range(2):
        c = a * SLOT
        x = to_slot(g_scr[a, :, :SLOT].astype(F32), 0)
        g0_ref[:, c : c + SLOT] = with_delta(x, o0[:, c : c + SLOT])
        x = to_slot(dot(picks[a, :n, :], g_scr[a], NN), HEAD_DIM)
        g1_ref[:, c : c + SLOT] = with_delta(x, o1[:, c : c + SLOT])


def own_backward_kernel(s0_ref, p_ref, g_ref, d_ref, ds_scr):
    tok = s0_ref.shape[0]
    for b in range(tok // SLOT):
        lo, hi = b * SLOT, (b + 1) * SLOT
        for a in range(2):
            at = a * SLOT
            v = s0_ref[:hi, 2 * PAIR + at : 2 * PAIR + at + SLOT]
            x = dot(v, g_ref[lo:hi, at : at + SLOT], NT)
            ds_scr[a, :hi, lo:hi] = (p_ref[a, :hi, lo:hi].astype(F32) * x).astype(BF16)
            if hi < tok:
                ds_scr[a, hi:, lo:hi] = jnp.zeros((tok - hi, SLOT), BF16)
    for a in range(2):
        at = a * SLOT
        q = s0_ref[:, at : at + SLOT]
        k = s0_ref[:, PAIR + at : PAIR + at + SLOT]
        ds = ds_scr[a]
        dq = dot(ds, k, TN) * SCALE
        dk = dot(ds, q, NN) * SCALE
        dv = clear(dot(p_ref[a], g_ref[:, at : at + SLOT], NN))
        d_ref[:, at : at + SLOT] = dq.astype(BF16)
        d_ref[:, PAIR + at : PAIR + at + SLOT] = dk.astype(BF16)
        d_ref[:, 2 * PAIR + at : 2 * PAIR + at + SLOT] = dv.astype(BF16)


def clear(x):
    return jnp.where(iota(x.shape, 1) < HEAD_DIM, x, 0.0)


def shifted_lanes(x, by):
    slot, by = by // SLOT, by % SLOT
    if by == 0:
        return slot, x
    if by + HEAD_DIM <= SLOT:
        return slot, pltpu.roll(x, by, 1)
    return slot, pltpu.roll(jnp.concatenate([x, jnp.zeros_like(x)], 1), by, 1)


def spread_matrix(offs, a, groups, tok):
    rows, _ = starts_of(tok)
    width = sum(rows[g] for g in groups)
    col = iota((1, width), 1)
    at = 0
    target = jnp.zeros((1, width), jnp.int32)
    for g in groups:
        here = (col - at) * (1 << g) + offs[GROUPS * a + g]
        target = jnp.where(col >= at, here, target) if at else here
        at += rows[g]
    return (iota((tok, width), 0) == target).astype(BF16)


def place_rows(b_scr, at, g, a, x):
    n = x.shape[0]
    slot, y = shifted_lanes(x, HEAD_DIM * g + a * (GROUPS * HEAD_DIM % SLOT))
    wide = y.shape[1] // SLOT
    zero = jnp.zeros((n, SLOT), BF16)
    for s in range(3):
        if slot <= s < slot + wide:
            part = y[:, (s - slot) * SLOT : (s - slot + 1) * SLOT].astype(BF16)
        else:
            part = zero
        b_scr[at : at + n, s * SLOT : (s + 1) * SLOT] = part


def store_halves(out_ref, halves, base=None):
    lo, hi = halves
    width = out_ref.shape[1]
    tiles = [lo[:, :SLOT], lo[:, SLOT:PAIR], lo[:, PAIR:] + hi[:, :SLOT]]
    tiles += [hi[:, SLOT:PAIR], hi[:, PAIR:]]
    for i, tile in enumerate(tiles):
        if base is not None:
            tile = tile + base[:, i * SLOT : (i + 1) * SLOT].astype(F32)
        out_ref[:, i * SLOT : (i + 1) * SLOT] = tile.astype(BF16)


def add_own(full, a, x):
    slot, y = shifted_lanes(x.astype(F32), a * (GROUPS * HEAD_DIM % SLOT))
    wide = y.shape[1]
    return jnp.concatenate([full[:, :wide] + y, full[:, wide:]], 1)


def query_kernel(spreads, d_ref, f_ref, g1_ref, g23_ref, q1, q2, q3, out_ref, b_scr):
    tok = out_ref.shape[0]
    rows, first = starts_of(tok)
    chain = [(g, a) for g in (1, 2, 3) for a in range(2)]
    pqs = {1: q1, 2: q2, 3: q3}
    grads = {}
    for g, a in chain:
        c = a * SLOT
        v = f_ref[g - 1, :, 2 * PAIR + c : 2 * PAIR + c + SLOT]
        at = first[g] - rows[1]
        gg = g1_ref[...] if g == 1 else g23_ref[at : at + rows[g], :]
        x = dot(gg[:, c : c + SLOT], v, NT)
        grads[g, a] = (pqs[g][a].astype(F32) * x).astype(BF16)
    for g, a in chain:
        k = f_ref[g - 1, :, PAIR + a * SLOT : PAIR + (a + 1) * SLOT]
        place_rows(b_scr.at[a], first[g], g, a, dot(grads[g, a], k, NN) * SCALE)
    halves = []
    for a in range(2):
        full = dot(spreads[a], b_scr[a], NN)
        halves.append(add_own(full, a, d_ref[:, a * SLOT : (a + 1) * SLOT]))
    store_halves(out_ref, halves)


def key_value_high_kernel(spreads, d_ref, f_ref, own, near, pk, key_ref, value_ref, g_scr, b_scr):
    tok = key_ref.shape[0]
    n = tok // 2
    g_scr[:n] = own[...]
    g_scr[n:] = near[...]
    key_value_rows((1,), tok, f_ref, (g_scr,), {1: pk}, b_scr)
    for i, out_ref in enumerate((key_ref, value_ref)):
        parts = []
        for a in range(2):
            c = (i + 1) * PAIR + a * SLOT
            x = dot(spreads[a, :, :n], b_scr[i, a], NN)
            parts.append(add_own(x, a, d_ref[:, c : c + SLOT]))
        store_halves(out_ref, parts)


def key_value_rows(groups, tok, f_ref, g_scr, pks, b_scr):
    rows, first = starts_of(tok)
    chain = [(g, a) for g in groups for a in range(2)]
    grads = {}
    for g, a in chain:
        c = a * SLOT
        v = f_ref[g - 1, : rows[g], 2 * PAIR + c : 2 * PAIR + c + SLOT]
        x = dot(v, g_scr[g - groups[0]][:, c : c + SLOT], NT)
        grads[g, a] = (pks[g][a].astype(F32) * x).astype(BF16)
    for g, a in chain:
        q = f_ref[g - 1, :, a * SLOT : (a + 1) * SLOT]
        at = first[g] - first[groups[0]]
        place_rows(b_scr.at[0, a], at, g, a, dot(grads[g, a], q, NN) * SCALE)
    for g, a in chain:
        gg = g_scr[g - groups[0]][:, a * SLOT : (a + 1) * SLOT]
        at = first[g] - first[groups[0]]
        place_rows(b_scr.at[1, a], at, g, a, clear(dot(pks[g][a], gg, NN)))


def key_value_low_kernel(
    spreads,
    query_in,
    key_in,
    value_in,
    f_ref,
    own,
    r2,
    r4,
    r6,
    d,
    k2,
    k3,
    query_out,
    key_out,
    value_out,
    g_scr,
    b_scr,
    key_scr,
    value_scr,
    sems,
):
    tok = key_scr.shape[0]
    n = tok // 2
    copies = [
        pltpu.make_async_copy(x, out, sems.at[i])
        for i, (x, out) in enumerate(
            ((query_in, query_out), (key_scr, key_out), (value_scr, value_out))
        )
    ]
    copies[0].start()
    for g in (2, 3):
        m, low = tok >> g, r2.shape[0]
        parts = parts_of(
            g,
            tok,
            (own, 0),
            (d, 0),
            (r2, 0),
            (d, low),
            (r4, 0),
            (r6, 0),
            (d, 2 * low),
            (d, 2 * low + r4.shape[0]),
        )
        for i, (ref, at) in enumerate(parts):
            g_scr[g - 2, i * m : (i + 1) * m, :] = ref[at : at + m, :]
    key_value_rows((2, 3), tok, f_ref, (g_scr.at[0], g_scr.at[1]), {2: k2, 3: k3}, b_scr)
    for i, (base, out) in enumerate(((key_in, key_scr), (value_in, value_scr))):
        parts = [dot(spreads[a, :, n:], b_scr[i, a], NN) for a in range(2)]
        store_halves(out, parts, base)
        copies[i + 1].start()
    for copy in copies:
        copy.wait()


VM = pl.BlockSpec(memory_space=pltpu.VMEM)
SM = pl.BlockSpec(memory_space=pltpu.SMEM)
HB = pl.BlockSpec(memory_space=pltpu.HBM)


def shape(*dims, dtype=BF16):
    return jax.ShapeDtypeStruct(dims, dtype)


def scratch(*dims, dtype=BF16):
    return pltpu.VMEM(dims, dtype)


def call(kernel, outs, operands, specs="", scratches=(), name=None, out=VM):
    kinds = {"s": SM, "h": HB, "v": VM}
    operands = [
        pltpu.with_memory_space_constraint(x, pltpu.HBM) if kind == "h" else x
        for x, kind in zip(operands, specs + "v" * len(operands))
    ]
    specs = [kinds[x] for x in specs]
    specs += [VM] * (len(operands) - len(specs))
    return pl.pallas_call(
        kernel,
        out_shape=outs,
        in_specs=specs,
        out_specs=jax.tree.map(lambda _: out, outs),
        scratch_shapes=list(scratches),
        compiler_params=pltpu.CompilerParams(vmem_limit_bytes=20 << 20),
        cost_estimate=pl.CostEstimate(
            flops=0, bytes_accessed=0, transcendentals=0
        ),
        name=name,
    )(*operands)


def on_device(queries, keys, values, out_grad, out_weight, offsets):
    tok, width = queries.shape
    rows, first = starts_of(tok)
    half = tok // 2
    index = lax.axis_index("seq")
    column = lax.axis_index("head")
    n_head = lax.axis_size("head")
    n_seq = lax.axis_size("seq")
    right_way = [(i, (i + 1) % n_head) for i in range(n_head)]
    left_way = [(i, (i - 1) % n_head) for i in range(n_head)]
    dma = pltpu.SemaphoreType.DMA

    def swap(x, mask):
        return lax.ppermute(x, "seq", [(i, i ^ mask) for i in range(n_seq)])

    def after(x, *others):
        return lax.optimization_barrier((x,) + others)[0]

    wide = 2 * HEAD_DIM
    n_all = sum(rows[1:])
    n_low = n_all - rows[1]

    left = lax.ppermute(out_grad, "head", right_way)
    right = lax.ppermute(out_grad, "head", left_way)

    blocks = [column, (column + n_head - 1) % n_head, (column + 1) % n_head]
    blocks += [(column + 2) % n_head, index]
    info = jnp.stack(blocks).astype(jnp.int32)

    s0, sall, s23, picks, spreads, own, wt = call(
        select_kernel,
        (
            shape(tok, 3 * PAIR),
            shape(n_all, 2 * PAIR),
            shape(n_low, 2 * PAIR),
            shape(2, n_all, tok),
            shape(2, tok, n_all),
            shape(tok, width),
            shape(4, width, width),
        ),
        (info, offsets, queries, keys, values, out_grad, out_weight),
        specs="shhhhhh",
        scratches=(scratch(3, tok, width), pltpu.SMEM((2 * GROUPS,), jnp.int32), dma((9,))),
        name="select",
    )

    def far_swaps(low):
        last = low[rows[2] :]
        r4 = swap(last, 4)
        r2 = swap(low, 2)
        return r2, r4, swap(last, 6)

    r2, r4, r6 = far_swaps(s23)
    acc_own = call(
        project_own_kernel,
        shape(4, tok, wide, dtype=F32),
        (own, wt),
        name="project_own",
    )
    p0, o0 = call(
        own_forward_kernel,
        (shape(2, tok, tok), shape(tok, PAIR, dtype=F32)),
        (s0,),
        name="own_forward",
    )
    left, right, acc_own, o0 = lax.optimization_barrier((left, right, acc_own, o0))
    far1 = lax.ppermute(left[:half], "head", right_way)
    far2 = lax.ppermute(right[half:], "head", left_way)
    r2, r4, r6, o0 = lax.optimization_barrier((r2, r4, r6, o0))
    near1 = swap(after(sall, o0)[: rows[1]], 1)
    da = swap(jnp.concatenate([s23, r6], 0), 1)
    db = swap(jnp.concatenate([r2, r4], 0), 1)
    acc = call(
        project_near_kernel,
        shape(4, tok, wide, dtype=F32),
        (after(acc_own, r2), left, right, wt),
        name="project_near",
    )
    seg = call(
        segment_forward_kernel,
        (shape(3, tok, 3 * PAIR), shape(rows[1], PAIR, dtype=F32), shape(n_low, PAIR, dtype=F32))
        + tuple(shape(2, rows[g], tok) for g in (1, 2, 3)) * 2,
        (info, sall, near1, da, r2, r4, r6, db),
        specs="s",
        name="segment_forward",
    )
    full, o1, o23 = seg[:3]
    pq, pk = seg[3:6], seg[6:9]

    pair_scratch = (scratch(tok, width), scratch(2, tok, PAIR))
    g23 = call(
        finish_low_kernel,
        shape(n_low, PAIR),
        (picks, acc, far1, far2, wt, o23),
        scratches=pair_scratch,
        name="finish_low",
    )
    g_far = far_swaps(g23)
    g0, g1 = call(
        finish_high_kernel,
        (shape(tok, PAIR), shape(rows[1], PAIR)),
        (picks, acc, far1, far2, wt, o0, o1),
        scratches=pair_scratch,
        name="finish_high",
    )
    g_near = swap(g1, 1)
    d0 = call(
        own_backward_kernel,
        shape(tok, 3 * PAIR),
        (s0, p0, g0),
        scratches=(scratch(2, tok, tok),),
        name="own_backward",
    )
    g_far = lax.optimization_barrier(g_far + (d0,))[:3]
    g_d = swap(jnp.concatenate((g23,) + g_far, 0), 1)
    key_part, value_part = call(
        key_value_high_kernel,
        (shape(tok, width), shape(tok, width)),
        (spreads, after(d0, g_far[1]), full, g1, g_near, pk[0]),
        scratches=(scratch(tok, PAIR), scratch(2, 2, rows[1], 3 * SLOT)),
        name="key_value_high",
    )
    query_part = call(
        query_kernel,
        shape(tok, width),
        (spreads, after(d0, g_far[1]), full, g1, g23) + tuple(pq),
        scratches=(scratch(2, n_all, 3 * SLOT),),
        name="query_side",
    )
    return tuple(
        call(
            key_value_low_kernel,
            (shape(tok, width),) * 3,
            (spreads, query_part, key_part, value_part, full, g23)
            + g_far
            + (g_d,)
            + tuple(pk[1:]),
            scratches=(
                scratch(2, tok, PAIR),
                scratch(2, 2, n_low, 3 * SLOT),
                scratch(tok, width),
                scratch(tok, width),
                dma((3,)),
            ),
            name="key_value_low",
            out=HB,
        )
    )


def solution(mesh):
    placed = (
        P("seq", "head"),
        P("seq", "head"),
        P("seq", "head"),
        P("seq", "head"),
        P("head", None),
        P("head"),
    )
    return jax.shard_map(
        on_device,
        mesh=mesh,
        in_specs=placed,
        out_specs=(P("seq", "head"), P("seq", "head"), P("seq", "head")),
        check_vma=False,
    )
```

```python
import functools

import jax
import jax.numpy as jnp
from jax import lax
from jax.experimental import pallas as pl
from jax.experimental.pallas import tpu as pltpu
from jax.sharding import PartitionSpec as P

HEAD_DIM = 80
GROUPS = 4
SLOT = 128
PAIR = 2 * SLOT
SPARE = SLOT - HEAD_DIM
NEG = -1e30
PLACE = 4
SCALE = HEAD_DIM ** (-0.5)
LOG2E = 1.4426950408889634
ORDER = {1: (0, 1), 2: (0, 1, 2, 3), 3: (0, 1, 2, 3, 4, 6, 5, 7)}
NT = (((1,), (1,)), ((), ()))
NN = (((1,), (0,)), ((), ()))
TN = (((0,), (0,)), ((), ()))
F32 = jnp.float32
BF16 = jnp.bfloat16


def dot(a, b, dims):
    return lax.dot_general(a, b, dims, preferred_element_type=F32)


def iota(shape, axis):
    return lax.broadcasted_iota(jnp.int32, shape, axis)


def window(head):
    low = HEAD_DIM * head
    start = low // SLOT * SLOT
    width = SLOT if low - start + HEAD_DIM <= SLOT else 2 * SLOT
    return start, width, low - start


def to_slot(x, shift, ones=0):
    if shift:
        x = pltpu.roll(x, x.shape[1] - shift, 1)
    x = x[:, :SLOT]
    lane = iota(x.shape, 1)
    fill = jnp.where(lane < HEAD_DIM + ones, 1.0, 0.0) if ones else 0.0
    return jnp.where(lane < HEAD_DIM, x, fill)


def pick(offset, rows, rate, tok):
    return (iota((rows, tok), 1) == iota((rows, tok), 0) * rate + offset).astype(BF16)


def starts_of(tok):
    rows = [tok >> g for g in range(GROUPS)]
    first = {g: sum(rows[1:g]) for g in range(1, GROUPS)}
    return rows, first


def select_kernel(
    info,
    offs_hbm,
    q_hbm,
    k_hbm,
    v_hbm,
    og_hbm,
    w_hbm,
    s0_ref,
    sall_ref,
    s23_ref,
    pick_scr,
    spread_ref,
    own_ref,
    wt_ref,
    x_scr,
    offs,
    sems,
):
    tok = x_scr.shape[1]
    width = x_scr.shape[2]
    rows, first = starts_of(tok)
    copies = [
        pltpu.make_async_copy(ref, x_scr.at[i], sems.at[i])
        for i, ref in enumerate((q_hbm, k_hbm, v_hbm))
    ]
    scalars = pltpu.make_async_copy(offs_hbm, offs, sems.at[3])
    copies.append(pltpu.make_async_copy(og_hbm, own_ref, sems.at[4]))
    for i in range(4):
        column = pl.ds(pl.multiple_of(info[i] * width, SLOT), width)
        copies.append(pltpu.make_async_copy(w_hbm.at[:, column], wt_ref.at[i], sems.at[5 + i]))
    scalars.start()
    for copy in copies:
        copy.start()
    scalars.wait()
    for a in range(2):
        spread_ref[a] = spread_matrix(offs, a, (1, 2, 3), tok)
        for g in range(1, GROUPS):
            chosen = pick(offs[GROUPS * a + g], rows[g], 1 << g, tok)
            pick_scr[a, first[g] : first[g] + rows[g], :] = chosen
    for i in range(3):
        copies[i].wait()
        for a in range(2):
            for g in range(GROUPS):
                start, width, shift = window(GROUPS * a + g)
                x = x_scr[i, :, start : start + width]
                if g == 0:
                    col = (2 * i + a) * SLOT
                    y = to_slot(x.astype(F32), shift, 2 if i == 2 else 0)
                    s0_ref[:, col : col + SLOT] = y.astype(BF16)
                    continue
                at, n = first[g], rows[g]
                y = to_slot(dot(pick_scr[a, at : at + n, :], x, NN), shift)
                if i < 2:
                    col = (2 * i + a) * SLOT
                    sall_ref[at : at + n, col : col + SLOT] = y.astype(BF16)
                    continue
                for half, by in ((0, HEAD_DIM), (1, HEAD_DIM - SPARE)):
                    col = (2 * a + half) * SLOT
                    spare = pltpu.roll(y, by, 1).astype(BF16)
                    lane = iota((n, SLOT), 1)
                    y_old = sall_ref[at : at + n, col : col + SLOT]
                    sall_ref[at : at + n, col : col + SLOT] = jnp.where(
                        lane < HEAD_DIM, y_old, spare
                    )
    s23_ref[...] = sall_ref[rows[1] :, :]
    for copy in copies[3:]:
        copy.wait()


def forward_block(q, k, mask):
    st = jnp.where(mask, dot(k, q, NT), NEG)
    top = jnp.max(st, axis=0, keepdims=True)
    e = jnp.exp2((st - top) * (SCALE * LOG2E))
    total = jnp.sum(e, axis=0, keepdims=True)
    return e * (1.0 / total)


def own_forward_kernel(s0_ref, p_ref, o_ref):
    tok = s0_ref.shape[0]
    for b in range(tok // SLOT):
        lo, hi = b * SLOT, (b + 1) * SLOT
        mask = iota((hi, SLOT), 0) <= iota((hi, SLOT), 1) + lo
        for a in range(2):
            at = a * SLOT
            q = s0_ref[lo:hi, at : at + SLOT]
            k = s0_ref[:hi, PAIR + at : PAIR + at + SLOT]
            v = s0_ref[:hi, 2 * PAIR + at : 2 * PAIR + at + SLOT]
            p = forward_block(q, k, mask).astype(BF16)
            p_ref[a, :hi, lo:hi] = p
            if hi < tok:
                p_ref[a, hi:, lo:hi] = jnp.zeros((tok - hi, SLOT), BF16)
            o_ref[lo:hi, at : at + SLOT] = dot(p, v, TN)


def parts_of(g, tok, own, near, r2, d2, r4, r6, d4, d6):
    rows, first = starts_of(tok)
    low = first[g] - rows[1]

    def at(source):
        return source[0], source[1] + low

    parts = [at(own), at(near), at(r2), at(d2)]
    return parts + [r4, r6, d4, d6] if g > 2 else parts


def unpack(out, at, x):
    n = x.shape[0]
    lane = iota((n, SLOT), 1)
    tiles = [x[:, i * SLOT : (i + 1) * SLOT].astype(F32) for i in range(4)]
    slots = [jnp.where(lane < HEAD_DIM, t, 0.0) for t in tiles]
    ones = jnp.where(lane < HEAD_DIM + 2, 1.0, 0.0)
    for a in range(2):
        low = pltpu.roll(tiles[2 * a], SPARE, 1)
        high = pltpu.roll(tiles[2 * a + 1], SLOT - HEAD_DIM + SPARE, 1)
        slots.append(jnp.where(lane < SPARE, low, jnp.where(lane < HEAD_DIM, high, ones)))
    for i, slot in enumerate(slots):
        out[at : at + n, i * SLOT : (i + 1) * SLOT] = slot.astype(BF16)


def places(g, n, place, shape, axis):
    s = iota(shape, axis)
    code = jnp.zeros(shape, jnp.int32)
    back = jnp.zeros(shape, jnp.int32)
    for i, m in enumerate(ORDER[g]):
        if i:
            code = jnp.where(s >= i * n, m, code)
            back = jnp.where(s >= i * n, i * n, back)
    return (code ^ place) * n + s - back


def segment_forward_kernel(
    info, own, near1, da, r2, r4, r6, db, f_ref, o1_ref, o23_ref, q1, q2, q3, k1, k2, k3
):
    tok = f_ref.shape[1]
    rows, first = starts_of(tok)
    for g, pq, pk in ((1, q1, k1), (2, q2, k2), (3, q3, k3)):
        n, low = rows[g], r2.shape[0]
        parts = [(own, 0), (near1, 0)]
        if g > 1:
            parts = parts_of(
                g, tok, (own, rows[1]), (da, 0), (r2, 0), (db, 0), (r4, 0), (r6, 0), (db, low), (da, low)
            )
        for i, (ref, at) in enumerate(parts):
            unpack(f_ref.at[g - 1], i * n, ref[at : at + n, :])
        place = lax.rem(info[PLACE], 1 << g)
        at_key = places(g, n, place, (tok, SLOT), 0)
        at_query = places(g, n, place, (1, tok), 1)
        for b in range(tok // SLOT):
            lo, hi = b * SLOT, (b + 1) * SLOT
            mask = at_key <= at_query[:, lo:hi]
            for a in range(2):
                c = a * SLOT
                q = f_ref[g - 1, lo:hi, c : c + SLOT]
                k = f_ref[g - 1, :, PAIR + c : PAIR + c + SLOT]
                p = forward_block(q, k, mask)
                pk[a, :, lo:hi] = p[:n].astype(BF16)
                own_rows = min(n, hi) - lo
                if own_rows > 0:
                    mine = jnp.transpose(p)[:own_rows].astype(BF16)
                    pq[a, lo : lo + own_rows, :] = mine
                    v = f_ref[g - 1, :, 2 * PAIR + c : 2 * PAIR + c + SLOT]
                    o = dot(mine, v, NN)
                    if g == 1:
                        o1_ref[lo : lo + own_rows, c : c + SLOT] = o
                    else:
                        at = first[g] - rows[1] + lo
                        o23_ref[at : at + own_rows, c : c + SLOT] = o


def project_own_kernel(own, wt, acc):
    for b in range(4):
        lo = 2 * HEAD_DIM * b
        acc[b] = dot(own[...], wt[0, lo : lo + 2 * HEAD_DIM], NT)


def project_near_kernel(acc_in, left, right, wt, acc):
    for b in range(4):
        lo = 2 * HEAD_DIM * b
        acc[b] = (
            acc_in[b]
            + dot(left[...], wt[1, lo : lo + 2 * HEAD_DIM], NT)
            + dot(right[...], wt[2, lo : lo + 2 * HEAD_DIM], NT)
        )


def with_delta(g, o):
    delta = jnp.sum(g.astype(BF16).astype(F32) * o, axis=1, keepdims=True)
    high = delta.astype(BF16).astype(F32)
    lane = iota(g.shape, 1)
    g = jnp.where(lane == HEAD_DIM, -high, g)
    return jnp.where(lane == HEAD_DIM + 1, high - delta, g).astype(BF16)


def finish_pairs(b0, acc, far1, far2, wt, x_scr, g_scr):
    half = far1.shape[0]
    x_scr[:half] = far1[...]
    x_scr[half:] = far2[...]
    wide = 2 * HEAD_DIM
    parts = []
    for a in range(2):
        b = 2 * a + b0
        lo = wide * b
        parts.append(acc[b] + dot(x_scr[...], wt[3, lo : lo + wide], NT))
        g_scr[a, :, wide:] = jnp.zeros((2 * half, PAIR - wide), BF16)
    for a in range(2):
        g_scr[a, :, :wide] = parts[a].astype(BF16)


def finish_low_kernel(picks, acc, far1, far2, wt, o23, g23_ref, x_scr, g_scr):
    tok = x_scr.shape[0]
    rows, first = starts_of(tok)
    finish_pairs(1, acc, far1, far2, wt, x_scr, g_scr)
    for g in (2, 3):
        for a in range(2):
            c = a * SLOT
            at = first[g] - rows[1]
            n = rows[g]
            x = dot(picks[a, first[g] : first[g] + n, :], g_scr[a], NN)
            x = to_slot(x, HEAD_DIM * (g - 2))
            g23_ref[at : at + n, c : c + SLOT] = with_delta(x, o23[at : at + n, c : c + SLOT])


def finish_high_kernel(picks, acc, far1, far2, wt, o0, o1, g0_ref, g1_ref, x_scr, g_scr):
    tok = x_scr.shape[0]
    n = tok // 2
    finish_pairs(0, acc, far1, far2, wt, x_scr, g_scr)
    for a in range(2):
        c = a * SLOT
        x = to_slot(g_scr[a, :, :SLOT].astype(F32), 0)
        g0_ref[:, c : c + SLOT] = with_delta(x, o0[:, c : c + SLOT])
        x = to_slot(dot(picks[a, :n, :], g_scr[a], NN), HEAD_DIM)
        g1_ref[:, c : c + SLOT] = with_delta(x, o1[:, c : c + SLOT])


def own_backward_kernel(s0_ref, p_ref, g_ref, d_ref, ds_scr):
    tok = s0_ref.shape[0]
    for b in range(tok // SLOT):
        lo, hi = b * SLOT, (b + 1) * SLOT
        for a in range(2):
            at = a * SLOT
            v = s0_ref[:hi, 2 * PAIR + at : 2 * PAIR + at + SLOT]
            x = dot(v, g_ref[lo:hi, at : at + SLOT], NT)
            ds_scr[a, :hi, lo:hi] = (p_ref[a, :hi, lo:hi].astype(F32) * x).astype(BF16)
            if hi < tok:
                ds_scr[a, hi:, lo:hi] = jnp.zeros((tok - hi, SLOT), BF16)
    for a in range(2):
        at = a * SLOT
        q = s0_ref[:, at : at + SLOT]
        k = s0_ref[:, PAIR + at : PAIR + at + SLOT]
        ds = ds_scr[a]
        dq = dot(ds, k, TN) * SCALE
        dk = dot(ds, q, NN) * SCALE
        dv = clear(dot(p_ref[a], g_ref[:, at : at + SLOT], NN))
        d_ref[:, at : at + SLOT] = dq.astype(BF16)
        d_ref[:, PAIR + at : PAIR + at + SLOT] = dk.astype(BF16)
        d_ref[:, 2 * PAIR + at : 2 * PAIR + at + SLOT] = dv.astype(BF16)


def clear(x):
    return jnp.where(iota(x.shape, 1) < HEAD_DIM, x, 0.0)


def shifted_lanes(x, by):
    slot, by = by // SLOT, by % SLOT
    if by == 0:
        return slot, x
    if by + HEAD_DIM <= SLOT:
        return slot, pltpu.roll(x, by, 1)
    return slot, pltpu.roll(jnp.concatenate([x, jnp.zeros_like(x)], 1), by, 1)


def spread_matrix(offs, a, groups, tok):
    rows, _ = starts_of(tok)
    width = sum(rows[g] for g in groups)
    col = iota((1, width), 1)
    at = 0
    target = jnp.zeros((1, width), jnp.int32)
    for g in groups:
        here = (col - at) * (1 << g) + offs[GROUPS * a + g]
        target = jnp.where(col >= at, here, target) if at else here
        at += rows[g]
    return (iota((tok, width), 0) == target).astype(BF16)


def place_rows(b_scr, at, g, a, x):
    n = x.shape[0]
    slot, y = shifted_lanes(x, HEAD_DIM * g + a * (GROUPS * HEAD_DIM % SLOT))
    wide = y.shape[1] // SLOT
    zero = jnp.zeros((n, SLOT), BF16)
    for s in range(3):
        if slot <= s < slot + wide:
            part = y[:, (s - slot) * SLOT : (s - slot + 1) * SLOT].astype(BF16)
        else:
            part = zero
        b_scr[at : at + n, s * SLOT : (s + 1) * SLOT] = part


def store_halves(out_ref, halves, base=None):
    lo, hi = halves
    width = out_ref.shape[1]
    tiles = [lo[:, :SLOT], lo[:, SLOT:PAIR], lo[:, PAIR:] + hi[:, :SLOT]]
    tiles += [hi[:, SLOT:PAIR], hi[:, PAIR:]]
    for i, tile in enumerate(tiles):
        if base is not None:
            tile = tile + base[:, i * SLOT : (i + 1) * SLOT].astype(F32)
        out_ref[:, i * SLOT : (i + 1) * SLOT] = tile.astype(BF16)


def add_own(full, a, x):
    slot, y = shifted_lanes(x.astype(F32), a * (GROUPS * HEAD_DIM % SLOT))
    wide = y.shape[1]
    return jnp.concatenate([full[:, :wide] + y, full[:, wide:]], 1)


def query_kernel(spreads, d_ref, f_ref, g1_ref, g23_ref, q1, q2, q3, out_ref, b_scr):
    tok = out_ref.shape[0]
    rows, first = starts_of(tok)
    chain = [(g, a) for g in (1, 2, 3) for a in range(2)]
    pqs = {1: q1, 2: q2, 3: q3}
    grads = {}
    for g, a in chain:
        c = a * SLOT
        v = f_ref[g - 1, :, 2 * PAIR + c : 2 * PAIR + c + SLOT]
        at = first[g] - rows[1]
        gg = g1_ref[...] if g == 1 else g23_ref[at : at + rows[g], :]
        x = dot(gg[:, c : c + SLOT], v, NT)
        grads[g, a] = (pqs[g][a].astype(F32) * x).astype(BF16)
    for g, a in chain:
        k = f_ref[g - 1, :, PAIR + a * SLOT : PAIR + (a + 1) * SLOT]
        place_rows(b_scr.at[a], first[g], g, a, dot(grads[g, a], k, NN) * SCALE)
    halves = []
    for a in range(2):
        full = dot(spreads[a], b_scr[a], NN)
        halves.append(add_own(full, a, d_ref[:, a * SLOT : (a + 1) * SLOT]))
    store_halves(out_ref, halves)


def key_value_rows(groups, tok, f_ref, g_scr, pks, b_scr):
    rows, first = starts_of(tok)
    chain = [(g, a) for g in groups for a in range(2)]
    grads = {}
    for g, a in chain:
        c = a * SLOT
        v = f_ref[g - 1, : rows[g], 2 * PAIR + c : 2 * PAIR + c + SLOT]
        x = dot(v, g_scr[g - groups[0]][:, c : c + SLOT], NT)
        grads[g, a] = (pks[g][a].astype(F32) * x).astype(BF16)
    for g, a in chain:
        q = f_ref[g - 1, :, a * SLOT : (a + 1) * SLOT]
        at = first[g] - first[groups[0]]
        place_rows(b_scr.at[0, a], at, g, a, dot(grads[g, a], q, NN) * SCALE)
    for g, a in chain:
        gg = g_scr[g - groups[0]][:, a * SLOT : (a + 1) * SLOT]
        at = first[g] - first[groups[0]]
        place_rows(b_scr.at[1, a], at, g, a, clear(dot(pks[g][a], gg, NN)))


def key_value_kernel(
    spreads,
    query_in,
    d_ref,
    f_ref,
    own1,
    own,
    r2,
    r4,
    r6,
    d,
    k1,
    k2,
    k3,
    query_out,
    key_out,
    value_out,
    g_scr,
    b_scr,
    key_scr,
    value_scr,
    sems,
):
    tok = key_scr.shape[0]
    n, low = own1.shape[0], own.shape[0]
    copies = [
        pltpu.make_async_copy(x, out, sems.at[i])
        for i, (x, out) in enumerate(
            ((query_in, query_out), (key_scr, key_out), (value_scr, value_out))
        )
    ]
    copies[0].start()
    for g in (1, 2, 3):
        m = tok >> g
        parts = [(own1, 0), (d, 0)]
        if g > 1:
            parts = parts_of(
                g,
                tok,
                (own, 0),
                (d, n),
                (r2, 0),
                (d, n + low),
                (r4, 0),
                (r6, 0),
                (d, n + 2 * low),
                (d, n + 2 * low + r4.shape[0]),
            )
        for i, (ref, at) in enumerate(parts):
            g_scr[g - 1, i * m : (i + 1) * m, :] = ref[at : at + m, :]
    g_refs = tuple(g_scr.at[i] for i in range(3))
    key_value_rows((1, 2, 3), tok, f_ref, g_refs, {1: k1, 2: k2, 3: k3}, b_scr)
    for i, out in enumerate((key_scr, value_scr)):
        parts = []
        for a in range(2):
            c = (i + 1) * PAIR + a * SLOT
            parts.append(add_own(dot(spreads[a], b_scr[i, a], NN), a, d_ref[:, c : c + SLOT]))
        store_halves(out, parts)
        copies[i + 1].start()
    for copy in copies:
        copy.wait()


VM = pl.BlockSpec(memory_space=pltpu.VMEM)
SM = pl.BlockSpec(memory_space=pltpu.SMEM)
HB = pl.BlockSpec(memory_space=pltpu.HBM)


def shape(*dims, dtype=BF16):
    return jax.ShapeDtypeStruct(dims, dtype)


def scratch(*dims, dtype=BF16):
    return pltpu.VMEM(dims, dtype)


def call(kernel, outs, operands, specs="", scratches=(), name=None, out=VM):
    kinds = {"s": SM, "h": HB, "v": VM}
    operands = [
        pltpu.with_memory_space_constraint(x, pltpu.HBM) if kind == "h" else x
        for x, kind in zip(operands, specs + "v" * len(operands))
    ]
    specs = [kinds[x] for x in specs]
    specs += [VM] * (len(operands) - len(specs))
    return pl.pallas_call(
        kernel,
        out_shape=outs,
        in_specs=specs,
        out_specs=jax.tree.map(lambda _: out, outs),
        scratch_shapes=list(scratches),
        compiler_params=pltpu.CompilerParams(vmem_limit_bytes=20 << 20),
        cost_estimate=pl.CostEstimate(
            flops=0, bytes_accessed=0, transcendentals=0
        ),
        name=name,
    )(*operands)


def on_device(queries, keys, values, out_grad, out_weight, offsets):
    tok, width = queries.shape
    rows, first = starts_of(tok)
    half = tok // 2
    index = lax.axis_index("seq")
    column = lax.axis_index("head")
    n_head = lax.axis_size("head")
    n_seq = lax.axis_size("seq")
    right_way = [(i, (i + 1) % n_head) for i in range(n_head)]
    left_way = [(i, (i - 1) % n_head) for i in range(n_head)]
    dma = pltpu.SemaphoreType.DMA

    def swap(x, mask):
        return lax.ppermute(x, "seq", [(i, i ^ mask) for i in range(n_seq)])

    def after(x, *others):
        return lax.optimization_barrier((x,) + others)[0]

    wide = 2 * HEAD_DIM
    n_all = sum(rows[1:])
    n_low = n_all - rows[1]

    left = lax.ppermute(out_grad, "head", right_way)
    right = lax.ppermute(out_grad, "head", left_way)

    blocks = [column, (column + n_head - 1) % n_head, (column + 1) % n_head]
    blocks += [(column + 2) % n_head, index]
    info = jnp.stack(blocks).astype(jnp.int32)

    s0, sall, s23, picks, spreads, own, wt = call(
        select_kernel,
        (
            shape(tok, 3 * PAIR),
            shape(n_all, 2 * PAIR),
            shape(n_low, 2 * PAIR),
            shape(2, n_all, tok),
            shape(2, tok, n_all),
            shape(tok, width),
            shape(4, width, width),
        ),
        (info, offsets, queries, keys, values, out_grad, out_weight),
        specs="shhhhhh",
        scratches=(scratch(3, tok, width), pltpu.SMEM((2 * GROUPS,), jnp.int32), dma((9,))),
        name="select",
    )

    def far_swaps(low):
        last = low[rows[2] :]
        r4 = swap(last, 4)
        r2 = swap(low, 2)
        return r2, r4, swap(last, 6)

    r2, r4, r6 = far_swaps(s23)
    acc_own = call(
        project_own_kernel,
        shape(4, tok, wide, dtype=F32),
        (own, wt),
        name="project_own",
    )
    p0, o0 = call(
        own_forward_kernel,
        (shape(2, tok, tok), shape(tok, PAIR, dtype=F32)),
        (s0,),
        name="own_forward",
    )
    left, right, acc_own, o0 = lax.optimization_barrier((left, right, acc_own, o0))
    far1 = lax.ppermute(left[:half], "head", right_way)
    far2 = lax.ppermute(right[half:], "head", left_way)
    r2, r4, r6, o0 = lax.optimization_barrier((r2, r4, r6, o0))
    near1 = swap(after(sall, o0)[: rows[1]], 1)
    da = swap(jnp.concatenate([s23, r6], 0), 1)
    db = swap(jnp.concatenate([r2, r4], 0), 1)
    acc = call(
        project_near_kernel,
        shape(4, tok, wide, dtype=F32),
        (after(acc_own, r2), left, right, wt),
        name="project_near",
    )
    seg = call(
        segment_forward_kernel,
        (shape(3, tok, 3 * PAIR), shape(rows[1], PAIR, dtype=F32), shape(n_low, PAIR, dtype=F32))
        + tuple(shape(2, rows[g], tok) for g in (1, 2, 3)) * 2,
        (info, sall, near1, da, r2, r4, r6, db),
        specs="s",
        name="segment_forward",
    )
    full, o1, o23 = seg[:3]
    pq, pk = seg[3:6], seg[6:9]

    pair_scratch = (scratch(tok, width), scratch(2, tok, PAIR))
    g23 = call(
        finish_low_kernel,
        shape(n_low, PAIR),
        (picks, acc, far1, far2, wt, o23),
        scratches=pair_scratch,
        name="finish_low",
    )
    g_far = far_swaps(g23)
    g0, g1 = call(
        finish_high_kernel,
        (shape(tok, PAIR), shape(rows[1], PAIR)),
        (picks, acc, far1, far2, wt, o0, o1),
        scratches=pair_scratch,
        name="finish_high",
    )
    d0 = call(
        own_backward_kernel,
        shape(tok, 3 * PAIR),
        (s0, p0, g0),
        scratches=(scratch(2, tok, tok),),
        name="own_backward",
    )
    query_part = call(
        query_kernel,
        shape(tok, width),
        (spreads, d0, full, g1, g23) + tuple(pq),
        scratches=(scratch(2, n_all, 3 * SLOT),),
        name="query_side",
    )
    g_far = lax.optimization_barrier(g_far + (query_part,))[:3]
    g_d = swap(jnp.concatenate((g1, g23) + g_far, 0), 1)
    return tuple(
        call(
            key_value_kernel,
            (shape(tok, width),) * 3,
            (spreads, query_part, d0, full, g1, g23)
            + g_far
            + (g_d,)
            + tuple(pk),
            scratches=(
                scratch(3, tok, PAIR),
                scratch(2, 2, n_all, 3 * SLOT),
                scratch(tok, width),
                scratch(tok, width),
                dma((3,)),
            ),
            name="key_value",
            out=HB,
        )
    )


def solution(mesh):
    placed = (
        P("seq", "head"),
        P("seq", "head"),
        P("seq", "head"),
        P("seq", "head"),
        P("head", None),
        P("head"),
    )
    return jax.shard_map(
        on_device,
        mesh=mesh,
        in_specs=placed,
        out_specs=(P("seq", "head"), P("seq", "head"), P("seq", "head")),
        check_vma=False,
    )
```

```python
import functools

import jax
import jax.numpy as jnp
from jax import lax
from jax.experimental import pallas as pl
from jax.experimental.pallas import tpu as pltpu
from jax.sharding import PartitionSpec as P

HEAD_DIM = 80
GROUPS = 4
SLOT = 128
PAIR = 2 * SLOT
SPARE = SLOT - HEAD_DIM
NEG = -1e30
PLACE = 4
SCALE = HEAD_DIM ** (-0.5)
LOG2E = 1.4426950408889634
ORDER = {1: (0, 1), 2: (0, 1, 2, 3), 3: (0, 1, 2, 3, 4, 6, 5, 7)}
NT = (((1,), (1,)), ((), ()))
NN = (((1,), (0,)), ((), ()))
TN = (((0,), (0,)), ((), ()))
F32 = jnp.float32
BF16 = jnp.bfloat16


def dot(a, b, dims):
    return lax.dot_general(a, b, dims, preferred_element_type=F32)


def iota(shape, axis):
    return lax.broadcasted_iota(jnp.int32, shape, axis)


def window(head):
    low = HEAD_DIM * head
    start = low // SLOT * SLOT
    width = SLOT if low - start + HEAD_DIM <= SLOT else 2 * SLOT
    return start, width, low - start


def to_slot(x, shift, ones=0):
    if shift:
        x = pltpu.roll(x, x.shape[1] - shift, 1)
    x = x[:, :SLOT]
    lane = iota(x.shape, 1)
    fill = jnp.where(lane < HEAD_DIM + ones, 1.0, 0.0) if ones else 0.0
    return jnp.where(lane < HEAD_DIM, x, fill)


def pick(offset, rows, rate, tok):
    return (iota((rows, tok), 1) == iota((rows, tok), 0) * rate + offset).astype(BF16)


def starts_of(tok):
    rows = [tok >> g for g in range(GROUPS)]
    first = {g: sum(rows[1:g]) for g in range(1, GROUPS)}
    return rows, first


def select_kernel(
    info,
    offs_hbm,
    q_hbm,
    k_hbm,
    v_hbm,
    og_hbm,
    w_hbm,
    s0_ref,
    sall_ref,
    s23_ref,
    pick_scr,
    spread_ref,
    own_ref,
    wt_ref,
    x_scr,
    offs,
    sems,
):
    tok = x_scr.shape[1]
    width = x_scr.shape[2]
    rows, first = starts_of(tok)
    copies = [
        pltpu.make_async_copy(ref, x_scr.at[i], sems.at[i])
        for i, ref in enumerate((q_hbm, k_hbm, v_hbm))
    ]
    scalars = pltpu.make_async_copy(offs_hbm, offs, sems.at[3])
    copies.append(pltpu.make_async_copy(og_hbm, own_ref, sems.at[4]))
    for i in range(4):
        column = pl.ds(pl.multiple_of(info[i] * width, SLOT), width)
        copies.append(pltpu.make_async_copy(w_hbm.at[:, column], wt_ref.at[i], sems.at[5 + i]))
    scalars.start()
    for copy in copies:
        copy.start()
    scalars.wait()
    for a in range(2):
        spread_ref[a] = spread_matrix(offs, a, (1, 2, 3), tok)
        for g in range(1, GROUPS):
            chosen = pick(offs[GROUPS * a + g], rows[g], 1 << g, tok)
            pick_scr[a, first[g] : first[g] + rows[g], :] = chosen
    for i in range(3):
        copies[i].wait()
        for a in range(2):
            for g in range(GROUPS):
                start, width, shift = window(GROUPS * a + g)
                x = x_scr[i, :, start : start + width]
                if g == 0:
                    col = (2 * i + a) * SLOT
                    y = to_slot(x.astype(F32), shift, 2 if i == 2 else 0)
                    s0_ref[:, col : col + SLOT] = y.astype(BF16)
                    continue
                at, n = first[g], rows[g]
                y = to_slot(dot(pick_scr[a, at : at + n, :], x, NN), shift)
                if i < 2:
                    col = (2 * i + a) * SLOT
                    sall_ref[at : at + n, col : col + SLOT] = y.astype(BF16)
                    continue
                for half, by in ((0, HEAD_DIM), (1, HEAD_DIM - SPARE)):
                    col = (2 * a + half) * SLOT
                    spare = pltpu.roll(y, by, 1).astype(BF16)
                    lane = iota((n, SLOT), 1)
                    y_old = sall_ref[at : at + n, col : col + SLOT]
                    sall_ref[at : at + n, col : col + SLOT] = jnp.where(
                        lane < HEAD_DIM, y_old, spare
                    )
    s23_ref[...] = sall_ref[rows[1] :, :]
    for copy in copies[3:]:
        copy.wait()


def forward_block(q, k, mask):
    st = jnp.where(mask, dot(k, q, NT), NEG)
    top = jnp.max(st, axis=0, keepdims=True)
    e = jnp.exp2((st - top) * (SCALE * LOG2E))
    total = jnp.sum(e, axis=0, keepdims=True)
    return e * (1.0 / total)


def own_forward_kernel(s0_ref, p_ref, o_ref):
    tok = s0_ref.shape[0]
    for b in range(tok // SLOT):
        lo, hi = b * SLOT, (b + 1) * SLOT
        mask = iota((hi, SLOT), 0) <= iota((hi, SLOT), 1) + lo
        for a in range(2):
            at = a * SLOT
            q = s0_ref[lo:hi, at : at + SLOT]
            k = s0_ref[:hi, PAIR + at : PAIR + at + SLOT]
            v = s0_ref[:hi, 2 * PAIR + at : 2 * PAIR + at + SLOT]
            p = forward_block(q, k, mask).astype(BF16)
            p_ref[a, :hi, lo:hi] = p
            if hi < tok:
                p_ref[a, hi:, lo:hi] = jnp.zeros((tok - hi, SLOT), BF16)
            o_ref[lo:hi, at : at + SLOT] = dot(p, v, TN)


def parts_of(g, tok, own, near, r2, d2, r4, r6, d4, d6):
    rows, first = starts_of(tok)
    low = first[g] - rows[1]

    def at(source):
        return source[0], source[1] + low

    parts = [at(own), at(near), at(r2), at(d2)]
    return parts + [r4, r6, d4, d6] if g > 2 else parts


def unpack(out, at, x):
    n = x.shape[0]
    lane = iota((n, SLOT), 1)
    tiles = [x[:, i * SLOT : (i + 1) * SLOT].astype(F32) for i in range(4)]
    slots = [jnp.where(lane < HEAD_DIM, t, 0.0) for t in tiles[:2]] + [None, None]
    ones = jnp.where(lane < HEAD_DIM + 2, 1.0, 0.0)
    for a in range(2):
        low = pltpu.roll(tiles[2 * a], SPARE, 1)
        high = pltpu.roll(tiles[2 * a + 1], SLOT - HEAD_DIM + SPARE, 1)
        slots.append(jnp.where(lane < SPARE, low, jnp.where(lane < HEAD_DIM, high, ones)))
    out[at : at + n, PAIR : 2 * PAIR] = x[:, PAIR:]
    for i, slot in enumerate(slots):
        if slot is not None:
            out[at : at + n, i * SLOT : (i + 1) * SLOT] = slot.astype(BF16)


def places(g, n, place, shape, axis):
    s = iota(shape, axis)
    code = jnp.zeros(shape, jnp.int32)
    back = jnp.zeros(shape, jnp.int32)
    for i, m in enumerate(ORDER[g]):
        if i:
            code = jnp.where(s >= i * n, m, code)
            back = jnp.where(s >= i * n, i * n, back)
    return (code ^ place) * n + s - back


def segment_forward_kernel(
    info, own, near1, da, r2, r4, r6, db, f_ref, o1_ref, o23_ref, q1, q2, q3, k1, k2, k3
):
    tok = f_ref.shape[1]
    rows, first = starts_of(tok)
    for g, pq, pk in ((1, q1, k1), (2, q2, k2), (3, q3, k3)):
        n, low = rows[g], r2.shape[0]
        parts = [(own, 0), (near1, 0)]
        if g > 1:
            parts = parts_of(
                g, tok, (own, rows[1]), (da, 0), (r2, 0), (db, 0), (r4, 0), (r6, 0), (db, low), (da, low)
            )
        for i, (ref, at) in enumerate(parts):
            unpack(f_ref.at[g - 1], i * n, ref[at : at + n, :])
        place = lax.rem(info[PLACE], 1 << g)
        at_key = jnp.concatenate(
            [iota((n, SLOT), 0) + (place ^ m) * n for m in ORDER[g]], 0
        )
        at_query = places(g, n, place, (1, tok), 1)
        for b in range(tok // SLOT):
            lo, hi = b * SLOT, (b + 1) * SLOT
            mask = at_key <= at_query[:, lo:hi]
            for a in range(2):
                c = a * SLOT
                q = f_ref[g - 1, lo:hi, c : c + SLOT]
                k = f_ref[g - 1, :, PAIR + c : PAIR + c + SLOT]
                p = forward_block(q, k, mask)
                pk[a, :, lo:hi] = p[:n].astype(BF16)
                own_rows = min(n, hi) - lo
                if own_rows > 0:
                    mine = jnp.transpose(p)[:own_rows].astype(BF16)
                    pq[a, lo : lo + own_rows, :] = mine
                    v = f_ref[g - 1, :, 2 * PAIR + c : 2 * PAIR + c + SLOT]
                    o = dot(mine, v, NN)
                    if g == 1:
                        o1_ref[lo : lo + own_rows, c : c + SLOT] = o
                    else:
                        at = first[g] - rows[1] + lo
                        o23_ref[at : at + own_rows, c : c + SLOT] = o


def project_own_kernel(own, wt, acc):
    for b in range(4):
        lo = 2 * HEAD_DIM * b
        acc[b] = dot(own[...], wt[0, lo : lo + 2 * HEAD_DIM], NT)


def project_near_kernel(acc_in, left, right, wt, acc):
    for b in range(4):
        lo = 2 * HEAD_DIM * b
        acc[b] = (
            acc_in[b]
            + dot(left[...], wt[1, lo : lo + 2 * HEAD_DIM], NT)
            + dot(right[...], wt[2, lo : lo + 2 * HEAD_DIM], NT)
        )


def with_delta(g, o):
    delta = jnp.sum(g.astype(BF16).astype(F32) * o, axis=1, keepdims=True)
    high = delta.astype(BF16).astype(F32)
    lane = iota(g.shape, 1)
    g = jnp.where(lane == HEAD_DIM, -high, g)
    return jnp.where(lane == HEAD_DIM + 1, high - delta, g).astype(BF16)


def finish_pairs(b0, acc, far1, far2, wt, x_scr, g_scr):
    half = far1.shape[0]
    x_scr[:half] = far1[...]
    x_scr[half:] = far2[...]
    wide = 2 * HEAD_DIM
    parts = []
    for a in range(2):
        b = 2 * a + b0
        lo = wide * b
        parts.append(acc[b] + dot(x_scr[...], wt[3, lo : lo + wide], NT))
        g_scr[a, :, wide:] = jnp.zeros((2 * half, PAIR - wide), BF16)
    for a in range(2):
        g_scr[a, :, :wide] = parts[a].astype(BF16)


def finish_low_kernel(picks, acc, far1, far2, wt, o23, g23_ref, x_scr, g_scr):
    tok = x_scr.shape[0]
    rows, first = starts_of(tok)
    finish_pairs(1, acc, far1, far2, wt, x_scr, g_scr)
    for g in (2, 3):
        for a in range(2):
            c = a * SLOT
            at = first[g] - rows[1]
            n = rows[g]
            x = dot(picks[a, first[g] : first[g] + n, :], g_scr[a], NN)
            x = to_slot(x, HEAD_DIM * (g - 2))
            g23_ref[at : at + n, c : c + SLOT] = with_delta(x, o23[at : at + n, c : c + SLOT])


def finish_high_kernel(picks, acc, far1, far2, wt, o0, o1, g0_ref, g1_ref, x_scr, g_scr):
    tok = x_scr.shape[0]
    n = tok // 2
    finish_pairs(0, acc, far1, far2, wt, x_scr, g_scr)
    for a in range(2):
        c = a * SLOT
        x = to_slot(g_scr[a, :, :SLOT].astype(F32), 0)
        g0_ref[:, c : c + SLOT] = with_delta(x, o0[:, c : c + SLOT])
        x = to_slot(dot(picks[a, :n, :], g_scr[a], NN), HEAD_DIM)
        g1_ref[:, c : c + SLOT] = with_delta(x, o1[:, c : c + SLOT])


def own_backward_kernel(s0_ref, p_ref, g_ref, d_ref, ds_scr):
    tok = s0_ref.shape[0]
    for b in range(tok // SLOT):
        lo, hi = b * SLOT, (b + 1) * SLOT
        for a in range(2):
            at = a * SLOT
            v = s0_ref[:hi, 2 * PAIR + at : 2 * PAIR + at + SLOT]
            x = dot(v, g_ref[lo:hi, at : at + SLOT], NT)
            ds_scr[a, :hi, lo:hi] = (p_ref[a, :hi, lo:hi].astype(F32) * x).astype(BF16)
            if hi < tok:
                ds_scr[a, hi:, lo:hi] = jnp.zeros((tok - hi, SLOT), BF16)
    for a in range(2):
        at = a * SLOT
        q = s0_ref[:, at : at + SLOT]
        k = s0_ref[:, PAIR + at : PAIR + at + SLOT]
        ds = ds_scr[a]
        dq = dot(ds, k, TN) * SCALE
        dk = dot(ds, q, NN) * SCALE
        dv = clear(dot(p_ref[a], g_ref[:, at : at + SLOT], NN))
        d_ref[:, at : at + SLOT] = dq.astype(BF16)
        d_ref[:, PAIR + at : PAIR + at + SLOT] = dk.astype(BF16)
        d_ref[:, 2 * PAIR + at : 2 * PAIR + at + SLOT] = dv.astype(BF16)


def clear(x):
    return jnp.where(iota(x.shape, 1) < HEAD_DIM, x, 0.0)


def shifted_lanes(x, by):
    slot, by = by // SLOT, by % SLOT
    if by == 0:
        return slot, x
    if by + HEAD_DIM <= SLOT:
        return slot, pltpu.roll(x, by, 1)
    return slot, pltpu.roll(jnp.concatenate([x, jnp.zeros_like(x)], 1), by, 1)


def spread_matrix(offs, a, groups, tok):
    rows, _ = starts_of(tok)
    width = sum(rows[g] for g in groups)
    col = iota((1, width), 1)
    at = 0
    target = jnp.zeros((1, width), jnp.int32)
    for g in groups:
        here = (col - at) * (1 << g) + offs[GROUPS * a + g]
        target = jnp.where(col >= at, here, target) if at else here
        at += rows[g]
    return (iota((tok, width), 0) == target).astype(BF16)


def place_rows(b_scr, at, g, a, x):
    n = x.shape[0]
    slot, y = shifted_lanes(x, HEAD_DIM * g + a * (GROUPS * HEAD_DIM % SLOT))
    wide = y.shape[1] // SLOT
    zero = jnp.zeros((n, SLOT), BF16)
    for s in range(3):
        if slot <= s < slot + wide:
            part = y[:, (s - slot) * SLOT : (s - slot + 1) * SLOT].astype(BF16)
        else:
            part = zero
        b_scr[at : at + n, s * SLOT : (s + 1) * SLOT] = part


def store_halves(out_ref, halves, base=None):
    lo, hi = halves
    width = out_ref.shape[1]
    tiles = [lo[:, :SLOT], lo[:, SLOT:PAIR], lo[:, PAIR:] + hi[:, :SLOT]]
    tiles += [hi[:, SLOT:PAIR], hi[:, PAIR:]]
    for i, tile in enumerate(tiles):
        if base is not None:
            tile = tile + base[:, i * SLOT : (i + 1) * SLOT].astype(F32)
        out_ref[:, i * SLOT : (i + 1) * SLOT] = tile.astype(BF16)


def add_own(full, a, x):
    slot, y = shifted_lanes(x.astype(F32), a * (GROUPS * HEAD_DIM % SLOT))
    wide = y.shape[1]
    return jnp.concatenate([full[:, :wide] + y, full[:, wide:]], 1)


def query_kernel(spreads, d_ref, f_ref, g1_ref, g23_ref, q1, q2, q3, out_ref, b_scr):
    tok = out_ref.shape[0]
    rows, first = starts_of(tok)
    chain = [(g, a) for g in (1, 2, 3) for a in range(2)]
    pqs = {1: q1, 2: q2, 3: q3}
    grads = {}
    for g, a in chain:
        c = a * SLOT
        v = f_ref[g - 1, :, 2 * PAIR + c : 2 * PAIR + c + SLOT]
        at = first[g] - rows[1]
        gg = g1_ref[...] if g == 1 else g23_ref[at : at + rows[g], :]
        x = dot(gg[:, c : c + SLOT], v, NT)
        grads[g, a] = (pqs[g][a].astype(F32) * x).astype(BF16)
    for g, a in chain:
        k = f_ref[g - 1, :, PAIR + a * SLOT : PAIR + (a + 1) * SLOT]
        place_rows(b_scr.at[a], first[g], g, a, clear(dot(grads[g, a], k, NN) * SCALE))
    halves = []
    for a in range(2):
        full = dot(spreads[a], b_scr[a], NN)
        halves.append(add_own(full, a, d_ref[:, a * SLOT : (a + 1) * SLOT]))
    store_halves(out_ref, halves)


def key_value_rows(groups, tok, f_ref, g_scr, pks, b_scr):
    rows, first = starts_of(tok)
    chain = [(g, a) for g in groups for a in range(2)]
    grads = {}
    for g, a in chain:
        c = a * SLOT
        v = f_ref[g - 1, : rows[g], 2 * PAIR + c : 2 * PAIR + c + SLOT]
        x = dot(v, g_scr[g - groups[0]][:, c : c + SLOT], NT)
        grads[g, a] = (pks[g][a].astype(F32) * x).astype(BF16)
    for g, a in chain:
        q = f_ref[g - 1, :, a * SLOT : (a + 1) * SLOT]
        at = first[g] - first[groups[0]]
        place_rows(b_scr.at[0, a], at, g, a, dot(grads[g, a], q, NN) * SCALE)
    for g, a in chain:
        gg = g_scr[g - groups[0]][:, a * SLOT : (a + 1) * SLOT]
        at = first[g] - first[groups[0]]
        place_rows(b_scr.at[1, a], at, g, a, clear(dot(pks[g][a], gg, NN)))


def key_value_kernel(
    spreads,
    query_in,
    d_ref,
    f_ref,
    own1,
    own,
    r2,
    r4,
    r6,
    d,
    k1,
    k2,
    k3,
    query_out,
    key_out,
    value_out,
    g_scr,
    b_scr,
    key_scr,
    value_scr,
    sems,
):
    tok = key_scr.shape[0]
    n, low = own1.shape[0], own.shape[0]
    copies = [
        pltpu.make_async_copy(x, out, sems.at[i])
        for i, (x, out) in enumerate(
            ((query_in, query_out), (key_scr, key_out), (value_scr, value_out))
        )
    ]
    copies[0].start()
    for g in (1, 2, 3):
        m = tok >> g
        parts = [(own1, 0), (d, 0)]
        if g > 1:
            parts = parts_of(
                g,
                tok,
                (own, 0),
                (d, n),
                (r2, 0),
                (d, n + low),
                (r4, 0),
                (r6, 0),
                (d, n + 2 * low),
                (d, n + 2 * low + r4.shape[0]),
            )
        for i, (ref, at) in enumerate(parts):
            g_scr[g - 1, i * m : (i + 1) * m, :] = ref[at : at + m, :]
    g_refs = tuple(g_scr.at[i] for i in range(3))
    key_value_rows((1, 2, 3), tok, f_ref, g_refs, {1: k1, 2: k2, 3: k3}, b_scr)
    for i, out in enumerate((key_scr, value_scr)):
        parts = []
        for a in range(2):
            c = (i + 1) * PAIR + a * SLOT
            parts.append(add_own(dot(spreads[a], b_scr[i, a], NN), a, d_ref[:, c : c + SLOT]))
        store_halves(out, parts)
        copies[i + 1].start()
    for copy in copies:
        copy.wait()


VM = pl.BlockSpec(memory_space=pltpu.VMEM)
SM = pl.BlockSpec(memory_space=pltpu.SMEM)
HB = pl.BlockSpec(memory_space=pltpu.HBM)


def shape(*dims, dtype=BF16):
    return jax.ShapeDtypeStruct(dims, dtype)


def scratch(*dims, dtype=BF16):
    return pltpu.VMEM(dims, dtype)


def call(kernel, outs, operands, specs="", scratches=(), name=None, out=VM):
    kinds = {"s": SM, "h": HB, "v": VM}
    operands = [
        pltpu.with_memory_space_constraint(x, pltpu.HBM) if kind == "h" else x
        for x, kind in zip(operands, specs + "v" * len(operands))
    ]
    specs = [kinds[x] for x in specs]
    specs += [VM] * (len(operands) - len(specs))
    return pl.pallas_call(
        kernel,
        out_shape=outs,
        in_specs=specs,
        out_specs=jax.tree.map(lambda _: out, outs),
        scratch_shapes=list(scratches),
        compiler_params=pltpu.CompilerParams(vmem_limit_bytes=20 << 20),
        cost_estimate=pl.CostEstimate(
            flops=0, bytes_accessed=0, transcendentals=0
        ),
        name=name,
    )(*operands)


def on_device(queries, keys, values, out_grad, out_weight, offsets):
    tok, width = queries.shape
    rows, first = starts_of(tok)
    half = tok // 2
    index = lax.axis_index("seq")
    column = lax.axis_index("head")
    n_head = lax.axis_size("head")
    n_seq = lax.axis_size("seq")
    right_way = [(i, (i + 1) % n_head) for i in range(n_head)]
    left_way = [(i, (i - 1) % n_head) for i in range(n_head)]
    dma = pltpu.SemaphoreType.DMA

    def swap(x, mask):
        return lax.ppermute(x, "seq", [(i, i ^ mask) for i in range(n_seq)])

    def after(x, *others):
        return lax.optimization_barrier((x,) + others)[0]

    wide = 2 * HEAD_DIM
    n_all = sum(rows[1:])
    n_low = n_all - rows[1]

    left = lax.ppermute(out_grad, "head", right_way)
    right = lax.ppermute(out_grad, "head", left_way)

    blocks = [column, (column + n_head - 1) % n_head, (column + 1) % n_head]
    blocks += [(column + 2) % n_head, index]
    info = jnp.stack(blocks).astype(jnp.int32)

    s0, sall, s23, picks, spreads, own, wt = call(
        select_kernel,
        (
            shape(tok, 3 * PAIR),
            shape(n_all, 2 * PAIR),
            shape(n_low, 2 * PAIR),
            shape(2, n_all, tok),
            shape(2, tok, n_all),
            shape(tok, width),
            shape(4, width, width),
        ),
        (info, offsets, queries, keys, values, out_grad, out_weight),
        specs="shhhhhh",
        scratches=(scratch(3, tok, width), pltpu.SMEM((2 * GROUPS,), jnp.int32), dma((9,))),
        name="select",
    )

    def far_swaps(low):
        last = low[rows[2] :]
        r4 = swap(last, 4)
        r2 = swap(low, 2)
        return r2, r4, swap(last, 6)

    r2, r4, r6 = far_swaps(s23)
    acc_own = call(
        project_own_kernel,
        shape(4, tok, wide, dtype=F32),
        (own, wt),
        name="project_own",
    )
    p0, o0 = call(
        own_forward_kernel,
        (shape(2, tok, tok), shape(tok, PAIR, dtype=F32)),
        (s0,),
        name="own_forward",
    )
    left, right, acc_own, o0 = lax.optimization_barrier((left, right, acc_own, o0))
    far1 = lax.ppermute(left[:half], "head", right_way)
    far2 = lax.ppermute(right[half:], "head", left_way)
    r2, r4, r6, o0 = lax.optimization_barrier((r2, r4, r6, o0))
    near1 = swap(after(sall, o0)[: rows[1]], 1)
    da = swap(jnp.concatenate([s23, r6], 0), 1)
    db = swap(jnp.concatenate([r2, r4], 0), 1)
    acc = call(
        project_near_kernel,
        shape(4, tok, wide, dtype=F32),
        (after(acc_own, r2), left, right, wt),
        name="project_near",
    )
    seg = call(
        segment_forward_kernel,
        (shape(3, tok, 3 * PAIR), shape(rows[1], PAIR, dtype=F32), shape(n_low, PAIR, dtype=F32))
        + tuple(shape(2, rows[g], tok) for g in (1, 2, 3)) * 2,
        (info, sall, near1, da, r2, r4, r6, db),
        specs="s",
        name="segment_forward",
    )
    full, o1, o23 = seg[:3]
    pq, pk = seg[3:6], seg[6:9]

    pair_scratch = (scratch(tok, width), scratch(2, tok, PAIR))
    g23 = call(
        finish_low_kernel,
        shape(n_low, PAIR),
        (picks, acc, far1, far2, wt, o23),
        scratches=pair_scratch,
        name="finish_low",
    )
    g_far = far_swaps(g23)
    g0, g1 = call(
        finish_high_kernel,
        (shape(tok, PAIR), shape(rows[1], PAIR)),
        (picks, acc, far1, far2, wt, o0, o1),
        scratches=pair_scratch,
        name="finish_high",
    )
    d0 = call(
        own_backward_kernel,
        shape(tok, 3 * PAIR),
        (s0, p0, g0),
        scratches=(scratch(2, tok, tok),),
        name="own_backward",
    )
    query_part = call(
        query_kernel,
        shape(tok, width),
        (spreads, d0, full, g1, g23) + tuple(pq),
        scratches=(scratch(2, n_all, 3 * SLOT),),
        name="query_side",
    )
    g_far = lax.optimization_barrier(g_far + (query_part,))[:3]
    g_d = swap(jnp.concatenate((g1, g23) + g_far, 0), 1)
    return tuple(
        call(
            key_value_kernel,
            (shape(tok, width),) * 3,
            (spreads, query_part, d0, full, g1, g23)
            + g_far
            + (g_d,)
            + tuple(pk),
            scratches=(
                scratch(3, tok, PAIR),
                scratch(2, 2, n_all, 3 * SLOT),
                scratch(tok, width),
                scratch(tok, width),
                dma((3,)),
            ),
            name="key_value",
            out=HB,
        )
    )


def solution(mesh):
    placed = (
        P("seq", "head"),
        P("seq", "head"),
        P("seq", "head"),
        P("seq", "head"),
        P("head", None),
        P("head"),
    )
    return jax.shard_map(
        on_device,
        mesh=mesh,
        in_specs=placed,
        out_specs=(P("seq", "head"), P("seq", "head"), P("seq", "head")),
        check_vma=False,
    )
```
